128 devices in a mesh: dp: 16 (over x, y_hi, core), tensor: 8 (over y_lo, z).
Axes of the slice: x: 4, y: 4 (y_hi: 2, y_lo: 2; y = y_hi * 2 + y_lo), z: 4, core: 2. Of those that a mesh axis runs over, the one named last changes fastest.
Arguments:
- grad_values: bfloat16 [2048, 16384], P('tensor', 'dp'), may hold values from -448 to 448
- row_scale: float32 [2048], P('tensor'), may hold values from 0.0004 to 0.004
- gate_input: bfloat16 [2048, 26624], P('dp', 'tensor'), may hold values from -8 to 8
- up_input: bfloat16 [2048, 26624], P('dp', 'tensor'), may hold values from -6 to 6
- down_weight: bfloat16 [26624, 16384], P('tensor', 'dp'), may hold values from -0.0390625 to 0.0390625
Outputs:
- down_grad: float32 [26624, 16384], P('tensor', 'dp')
- gate_grad: bfloat16 [2048, 26624], P('dp', 'tensor')
- up_grad: bfloat16 [2048, 26624], P('dp', 'tensor')
The draws below stay inside these ranges and needn't reach their ends.
All inputs are finite; a program needn't handle non-finite values.
Results may differ from the reference program's by a relative error of at most 0.039.
Values may be sent and summed in bfloat16 or wider, within the bound.
A program may use at most 128 MiB of HBM per device.

```python
import math
import jax
import jax.numpy as jnp
from jax import lax

D = 16384
FF = 26624
TOKENS = 2048
N_DP = 16


def spiked(result, stream_key, source, target, parts, factor):
    def block_of(position):
        return (jnp.arange(result.shape[position]) // (result.shape[position] // parts)).reshape((-1,) + (1,) * (result.ndim - 1 - position))

    one_side = jax.random.permutation(stream_key, parts)[block_of(target)]
    far = (block_of(target) + parts // 2) % parts
    return jnp.where((block_of(source) == one_side) | (block_of(source) == far), factor * result, result)


def block_levels(rng, dims, shards, low, high):
    level = 1.0
    for position, shards_of in shards:
        steps = jax.random.uniform(jax.random.fold_in(jax.random.fold_in(rng, 6), position), (shards_of,), jnp.float32, low / len(shards), high / len(shards))
        level = level * jnp.repeat(jnp.exp(steps), dims[position] // shards_of).reshape((-1,) + (1,) * (len(dims) - 1 - position))
    return level


def gaussian(rng, shape, spread, most, shards=(), kind=jnp.bfloat16):
    drawn = jax.random.normal(rng, shape, jnp.float32) * spread
    if len(shards) > 0:
        drawn = block_levels(rng, shape, shards, -0.22, 0.18) * drawn
    return jnp.clip(drawn, min=-most, max=most).astype(kind)


def bell_draw_with(key, extent, scale, most, shards, heavy, kind=jnp.bfloat16):
    drawn = scale * jax.random.normal(key, extent, jnp.float32)
    if shards:
        drawn = drawn * block_levels(key, extent, shards, -0.22, 0.18)
    return jnp.clip(spiked(drawn, jax.random.fold_in(key, 3), *heavy), -most, most).astype(kind)


def setup_inputs(seed: int = 0) -> dict:
    seeds = jax.random.split(jax.random.key(seed), 6)
    grad_values = bell_draw_with(seeds[0], (TOKENS, D), 112.0, 448.0, ((0, 8), (1, 16)), (1, 0, 16, 2.0))
    row_scale = jnp.clip(jnp.exp(math.log(0.004) - 2.3025852 * jax.random.uniform(seeds[1], (TOKENS,), jnp.float32) ** block_levels(seeds[1], (TOKENS,), ((0, 8),), -0.2, 0.2)), 0.0004, 0.004)
    gate_input = gaussian(seeds[2], (TOKENS, FF), 1.5, 8.0, ((0, 16), (1, 8)))
    up_input = gaussian(seeds[3], (TOKENS, FF), 1.0, 6.0, ((0, 16), (1, 8)))
    down_weight = gaussian(seeds[4], (FF, D), FF ** -0.5, 0.0390625, ((0, 8), (1, 16)))
    return dict(grad_values=grad_values, row_scale=row_scale, gate_input=gate_input, up_input=up_input, down_weight=down_weight)


def reference(grad_values, row_scale, gate_input, up_input, down_weight):
    grad_out = (grad_values.astype(jnp.float32) * row_scale[:, None]).astype(jnp.bfloat16)
    gate_float = gate_input.astype(jnp.float32)
    up_float = up_input.astype(jnp.float32)
    sigmoid_gate = jax.nn.sigmoid(gate_float)
    activated = gate_float * sigmoid_gate
    hidden = (activated * up_float).astype(jnp.bfloat16)
    down_grad = lax.dot_general(hidden, grad_out, (((0,), (0,)), ((), ())), preferred_element_type=jnp.float32)
    col_width = D // N_DP

    def add_block(running, block_index):
        grad_cols = lax.dynamic_slice_in_dim(grad_out, block_index * col_width, col_width, 1)
        weight_cols = lax.dynamic_slice_in_dim(down_weight, block_index * col_width, col_width, 1)
        partial_value = lax.dot_general(grad_cols, weight_cols, (((1,), (1,)), ((), ())), preferred_element_type=jnp.float32)
        rounded = lax.optimization_barrier(partial_value.astype(jnp.bfloat16))
        return running + rounded.astype(jnp.float32), None

    start_sum = jnp.zeros((grad_out.shape[0], down_weight.shape[0]), jnp.float32)
    hidden_grad, _ = lax.scan(add_block, start_sum, jnp.arange(N_DP, dtype=jnp.int32))
    gate_grad = (hidden_grad * up_float * sigmoid_gate * (1.0 + gate_float * (1.0 - sigmoid_gate))).astype(jnp.bfloat16)
    up_grad = (hidden_grad * activated).astype(jnp.bfloat16)
    return (down_grad, gate_grad, up_grad)
```

```python
import functools

import jax
import jax.numpy as jnp
from jax import lax
from jax.experimental import pallas as pl
from jax.experimental.pallas import tpu as pltpu
from jax.sharding import PartitionSpec as P

MESH = pl.DeviceIdType.MESH
BF16 = jnp.bfloat16
F32 = jnp.float32

TOK = 2048
FFL = 3328
HALF = FFL // 2
DL = 1024
N1 = 1024
N2 = HALF - N1
N_COPIES = 96


class Copies:
    def __init__(self, send_sem, recv_sem):
        self.send_sem, self.recv_sem = send_sem, recv_sem
        self.sent = []

    def send(self, src, dst, device):
        index = len(self.sent)
        copy = pltpu.make_async_remote_copy(
            src_ref=src,
            dst_ref=dst,
            send_sem=self.send_sem.at[index],
            recv_sem=self.recv_sem.at[index],
            device_id=device,
            device_id_type=MESH,
        )
        copy.start()
        self.sent.append(copy)
        return index

    def arrived(self, index):
        self.sent[index].wait_recv()

    def finish(self):
        for copy in self.sent:
            copy.wait_send()


def kernel(
    values, scale, gate, up, weight,
    dg_out, gg_out, ug_out,
    g_all, w_both, h_all, p1, p2, r1a, r1b, r1y, r2y, r2a, r2b,
    hg, fin, v_in, gate_in, up_in, dg_buf,
    send_sem, recv_sem, load_sem, dg_sem,
):
    dp = lax.axis_index("dp")
    tensor = lax.axis_index("tensor")
    c = lax.rem(dp, 2)
    yh = lax.rem(dp // 2, 2)
    x = dp // 4
    yl = tensor // 4
    z = lax.rem(tensor, 4)
    q = dp // 2

    def wrap(i):
        return lax.rem(i + 4, 4)

    xr, xl, xf = wrap(x + 1), wrap(x - 1), wrap(x + 2)
    zr, zl, zf = wrap(z + 1), wrap(z - 1), wrap(z + 2)
    to_xr = (xr * 4 + yh * 2 + c, tensor)
    to_xl = (xl * 4 + yh * 2 + c, tensor)
    to_yh = (x * 4 + (1 - yh) * 2 + c, tensor)
    to_core = (q * 2 + (1 - c), tensor)
    to_yl = (dp, (1 - yl) * 4 + z)
    to_zr = (dp, yl * 4 + zr)
    to_zl = (dp, yl * 4 + zl)

    def chip(xx, yy):
        return xx * 2 + yy

    def load(i, src, dst):
        copy = pltpu.make_async_copy(src, dst, load_sem.at[i])
        copy.start()
        return copy

    own_half = pl.ds(pl.multiple_of(c * HALF, 128), HALF)
    sib_half = pl.ds(pl.multiple_of((1 - c) * HALF, 128), HALF)
    load_v = load(0, values, v_in)
    load_g = load(1, gate, gate_in)
    load_u = load(2, up, up_in)
    load_w = load(3, weight.at[own_half], w_both.at[c])

    barrier = pltpu.get_barrier_semaphore()
    for neighbour in (to_xr, to_xl, to_yh, to_core, to_yl, to_zr, to_zl):
        pl.semaphore_signal(barrier, inc=1, device_id=neighbour, device_id_type=MESH)
    pl.semaphore_wait(barrier, 7)

    net = Copies(send_sem, recv_sem)
    send, arrived = net.send, net.arrived

    def g_rows(block, first=0, rows=256):
        return g_all.at[c, pl.ds(pl.multiple_of(block * 256 + first, 128), rows)]

    def send_g(block, device, first=0, rows=256):
        ref = g_rows(block, first, rows)
        return send(ref, ref, device)

    load_v.wait()
    own = tensor
    for i in range(2):
        col = jnp.broadcast_to(scale[i : i + 1, :], (128, 128)).T
        for k in range(DL // 128):
            part = v_in[i * 128 : (i + 1) * 128, k * 128 : (k + 1) * 128].astype(F32) * col
            g_all[c, pl.ds(pl.multiple_of(own * 256 + i * 128, 128), 128), k * 128 : (k + 1) * 128] = part.astype(BF16)
    a_yl = send_g(own, to_yl)
    a_zr = send_g(own, to_zr)
    a_zl = send_g(own, to_zl)
    s_own = send_g(own, to_core)
    w_sib = send(weight.at[sib_half], w_both.at[c], to_core)

    load_g.wait()
    load_u.wait()

    def hidden_tile(k, _):
        cols = pl.ds(pl.multiple_of(k * 128, 128), 128)
        gate_f = gate_in[:, cols].astype(F32)
        h = gate_f * jax.nn.sigmoid(gate_f) * up_in[:, cols].astype(F32)
        h_all[dp, cols, :] = h.T.astype(BF16)
        return 0

    lax.fori_loop(0, FFL // 128, hidden_tile, 0, unroll=2)

    base = pl.multiple_of(c * HALF, 128)
    rows1 = pl.ds(base, N1)
    rows2 = pl.ds(pl.multiple_of(base + N1, 128), N2)

    def send_h(first, count, rows, device):
        ref = h_all.at[pl.ds(first, count), rows]
        return send(ref, ref, device)

    both = pl.ds(dp, 1)
    s_h = send(h_all.at[both], h_all.at[both], to_core)
    arrived(s_h)
    b1_y = send_h(2 * q, 2, rows1, to_yh)
    b2_xr = send_h(2 * q, 2, rows2, to_xr)
    b2_xl = send_h(2 * q, 2, rows2, to_xl)
    b1_xr = send_h(2 * q, 2, rows1, to_xr)
    b1_xl = send_h(2 * q, 2, rows1, to_xl)

    sib = []

    def share_h(first, count, rows):
        sib.append(send_h(first, count, rows, to_core))

    def product(block):
        rows = pl.ds(pl.multiple_of(block * 256, 256), 256)

        def cols_of(first, width):
            w_rows = pl.ds(first, width)
            total = lax.dot_general(
                g_all[0, rows, :], w_both[0, w_rows, :], (((1,), (1,)), ((), ())), preferred_element_type=F32
            )
            total += lax.dot_general(
                g_all[1, rows, :], w_both[1, w_rows, :], (((1,), (1,)), ((), ())), preferred_element_type=F32
            )
            return total.astype(BF16)

        def tile(n, _):
            first = pl.multiple_of(n * 256, 256)
            p1[block, :, pl.ds(first, 256)] = cols_of(first, 256)
            return 0

        lax.fori_loop(0, N1 // 256, tile, 0)
        p2[block, :, :] = cols_of(N1, N2)

    other = (1 - yl) * 4 + z
    arrived(a_yl)
    a_yzr = send_g(other, to_zr)
    a_yzl = send_g(other, to_zl)
    s_other = send_g(other, to_core)

    qy = chip(x, 1 - yh)
    arrived(b1_y)
    b1_yxr = send_h(2 * qy, 2, rows1, to_xr)
    b1_yxl = send_h(2 * qy, 2, rows1, to_xl)
    b2_y = send_h(2 * q, 2, rows2, to_yh)
    share_h(2 * qy, 2, rows1)

    arrived(a_zr)
    a_fr = send_g(yl * 4 + zl, to_zr, 0, 128)
    s_zl = send_g(yl * 4 + zl, to_core)
    arrived(a_zl)
    a_fl = send_g(yl * 4 + zr, to_zl, 128, 128)
    s_zr = send_g(yl * 4 + zr, to_core)

    ql, qr, qf = chip(xl, yh), chip(xr, yh), chip(xf, yh)
    arrived(b2_xr)
    b2_fr = send_h(2 * ql, 1, rows2, to_xr)
    b2_yl = send_h(2 * ql, 2, rows2, to_yh)
    share_h(2 * ql, 2, rows2)
    arrived(b2_xl)
    b2_fl = send_h(2 * qr + 1, 1, rows2, to_xl)
    b2_yr = send_h(2 * qr, 2, rows2, to_yh)
    share_h(2 * qr, 2, rows2)

    arrived(b1_xr)
    b1_fr = send_h(2 * ql, 1, rows1, to_xr)
    share_h(2 * ql, 2, rows1)
    arrived(b1_xl)
    b1_fl = send_h(2 * qr + 1, 1, rows1, to_xl)
    share_h(2 * qr, 2, rows1)

    load_w.wait()
    arrived(w_sib)
    arrived(s_own)
    arrived(s_other)

    def near(i, _):
        product(i * 4 + z)
        return 0

    lax.fori_loop(0, 2, near, 0)

    ol = (1 - yl) * 4 + zl
    orr = (1 - yl) * 4 + zr
    arrived(a_yzr)
    a_yfr = send_g(ol, to_zr, 0, 128)
    s_ol = send_g(ol, to_core)
    arrived(a_yzl)
    a_yfl = send_g(orr, to_zl, 128, 128)
    s_or = send_g(orr, to_core)

    arrived(b2_fr)
    arrived(b2_fl)
    b2_yf = send_h(2 * qf, 2, rows2, to_yh)
    share_h(2 * qf, 2, rows2)

    qyl, qyr, qyf = chip(xl, 1 - yh), chip(xr, 1 - yh), chip(xf, 1 - yh)
    arrived(b1_yxr)
    b1_yfr = send_h(2 * qyl, 1, rows1, to_xr)
    share_h(2 * qyl, 2, rows1)
    arrived(b1_yxl)
    b1_yfl = send_h(2 * qyr + 1, 1, rows1, to_xl)
    share_h(2 * qyr, 2, rows1)

    arrived(a_fr)
    arrived(a_fl)
    s_f = send_g(yl * 4 + zf, to_core)

    for s in (s_zl, s_zr, s_ol, s_or):
        arrived(s)

    def middle(i, _):
        product((i // 2) * 4 + wrap(z - 1 + 2 * lax.rem(i, 2)))
        return 0

    lax.fori_loop(0, 4, middle, 0)

    arrived(a_yfr)
    arrived(a_yfl)
    s_of = send_g((1 - yl) * 4 + zf, to_core)
    arrived(s_f)
    arrived(s_of)

    def far(i, _):
        product(i * 4 + zf)
        return 0

    lax.fori_loop(0, 2, far, 0)

    top, low = pl.ds(0, 128), pl.ds(128, 128)
    lows, tops = [], []
    for yy in range(2):
        bf = chip(xf, yy)
        lows.append(send(p1.at[bf, top], r1a.at[0, yy], to_xr))
        tops.append(send(p1.at[bf, low], r1a.at[1, yy], to_xl))
    c2y_f = send(p2.at[chip(xf, 1 - yh)], r2y.at[xf], to_yh)
    c2y_r = send(p2.at[chip(xr, 1 - yh)], r2y.at[xr], to_yh)
    c2y_l = send(p2.at[chip(xl, 1 - yh)], r2y.at[xl], to_yh)
    c2y_o = send(p2.at[chip(x, 1 - yh)], r2y.at[x], to_yh)
    c1 = [[], []]
    for yy in range(2):
        c1[yy].append(send(p1.at[chip(xr, yy), low], r1b.at[0, yy, low], to_xr))
        c1[yy].append(send(p1.at[chip(xl, yy), top], r1b.at[1, yy, top], to_xl))

    arrived(b1_fr)
    arrived(b1_fl)
    share_h(2 * qf, 2, rows1)
    arrived(b2_y)
    share_h(2 * qy, 2, rows2)
    arrived(b2_yl)
    share_h(2 * qyl, 2, rows2)
    arrived(b2_yr)
    share_h(2 * qyr, 2, rows2)

    def add(dst, rows, others):
        def strip(i, _):
            at = pl.ds(pl.multiple_of(rows[0] + i * 16, 16), 16)
            total = dst[at, :].astype(F32)
            for other_ref, shift in others:
                total += other_ref[pl.ds(pl.multiple_of(rows[0] - shift + i * 16, 16), 16), :].astype(F32)
            dst[at, :] = total.astype(BF16)
            return 0

        lax.fori_loop(0, rows[1] // 16, strip, 0)

    for yy in range(2):
        arrived(lows[yy])
        add(p1.at[chip(xr, yy)], (0, 128), [(r1a.at[0, yy], 0)])
        c1[yy].append(send(p1.at[chip(xr, yy), top], r1b.at[0, yy, top], to_xr))
        arrived(tops[yy])
        add(p1.at[chip(xl, yy)], (128, 128), [(r1a.at[1, yy], 128)])
        c1[yy].append(send(p1.at[chip(xl, yy), low], r1b.at[1, yy, low], to_xl))

    arrived(b1_yfr)
    arrived(b1_yfl)
    share_h(2 * qyf, 2, rows1)
    arrived(b2_yf)
    share_h(2 * qyf, 2, rows2)
    for s in sib:
        arrived(s)

    def dg_copy(slot, m):
        return pltpu.make_async_copy(
            dg_buf.at[slot], dg_out.at[pl.ds(pl.multiple_of(m * 128, 128), 128)], dg_sem.at[slot]
        )

    def dg_tile(m, _):
        slot = lax.rem(m, 2)

        @pl.when(m >= 2)
        def _():
            dg_copy(slot, m).wait()

        rows = pl.ds(pl.multiple_of(m * 128, 128), 128)
        lhs = jnp.concatenate([h_all[s, rows, :] for s in range(16)], axis=1)
        dg_buf[slot] = jnp.dot(lhs, g_all[c], preferred_element_type=F32)
        dg_copy(slot, m).start()
        return 0

    def down(first, last):
        lax.fori_loop(first, last, dg_tile, 0)

    down(0, 4)
    arrived(c2y_f)
    bf = chip(xf, yh)
    add(p2.at[bf], (0, 256), [(r2y.at[xf], 0)])
    c2a_r = send(p2.at[bf, top], r2a.at[0], to_xr)
    c2a_l = send(p2.at[bf, low], r2a.at[1], to_xl)
    down(4, 9)
    arrived(c2y_r)
    br, bl = chip(xr, yh), chip(xl, yh)
    add(p2.at[br], (128, 128), [(r2y.at[xr], 0)])
    c2_r = [send(p2.at[br, low], r2b.at[0, low], to_xr)]
    arrived(c2y_l)
    add(p2.at[bl], (0, 128), [(r2y.at[xl], 0)])
    c2_l = [send(p2.at[bl, top], r2b.at[1, top], to_xl)]
    arrived(c2a_r)
    add(p2.at[br], (0, 128), [(r2y.at[xr], 0), (r2a.at[0], 0)])
    c2_r.append(send(p2.at[br, top], r2b.at[0, top], to_xr))
    arrived(c2a_l)
    add(p2.at[bl], (128, 128), [(r2y.at[xl], 0), (r2a.at[1], 128)])
    c2_l.append(send(p2.at[bl, low], r2b.at[1, low], to_xl))
    down(9, 16)

    for s in c1[0] + c1[1]:
        arrived(s)
    bo = chip(x, 1 - yh)
    add(p1.at[bo], (0, 256), [(r1b.at[0, 1 - yh], 0), (r1b.at[1, 1 - yh], 0)])
    c1_y = send(p1.at[bo], r1y, to_yh)
    down(16, 26)

    own_rows = pl.multiple_of(c * 128, 128)
    sib_rows = pl.multiple_of((1 - c) * 128, 128)

    def total_of(first, dst, cols, terms):
        def strip(i, _):
            at = pl.ds(pl.multiple_of(first + i * 16, 16), 16)
            total = terms[0][at, :].astype(F32)
            for term in terms[1:]:
                total += term[at, :].astype(F32)
            dst[pl.ds(pl.multiple_of(i * 16, 16), 16), cols] = total
            return 0

        lax.fori_loop(0, 8, strip, 0)

    for s in c2_r + c2_l + [c2y_o]:
        arrived(s)
    terms2 = [p2.at[q], r2y.at[x], r2b.at[0], r2b.at[1]]
    terms1 = [p1.at[q], r1b.at[0, yh], r1b.at[1, yh], r1y]
    cols1, cols2 = slice(0, N1), slice(N1, HALF)
    total_of(sib_rows, fin, cols2, terms2)
    total_of(own_rows, hg.at[c], cols2, terms2)
    arrived(c1_y)
    total_of(sib_rows, fin, cols1, terms1)
    last = send(fin, hg.at[c], to_core)
    total_of(own_rows, hg.at[c], cols1, terms1)

    def finish_half(half):
        def strip(k, _):
            cols = pl.ds(pl.multiple_of(half * HALF + k * 128, 128), 128)
            grad = hg[half, :, pl.ds(pl.multiple_of(k * 128, 128), 128)]
            gate_f = gate_in[:, cols].astype(F32)
            s = jax.nn.sigmoid(gate_f)
            gg_out[:, cols] = (grad * up_in[:, cols].astype(F32) * s * (1.0 + gate_f * (1.0 - s))).astype(BF16)
            ug_out[:, cols] = (grad * (gate_f * s)).astype(BF16)
            return 0

        lax.fori_loop(0, HALF // 128, strip, 0)

    finish_half(c)
    arrived(last)
    finish_half(1 - c)

    for slot in range(2):
        dg_copy(slot, 24 + slot).wait()
    net.finish()


def body(grad_values, row_scale, gate_input, up_input, down_weight):
    any_spec = pl.BlockSpec(memory_space=pl.ANY)
    vmem_spec = pl.BlockSpec(memory_space=pltpu.VMEM)
    return pl.pallas_call(
        kernel,
        out_shape=(
            jax.ShapeDtypeStruct((FFL, DL), F32),
            jax.ShapeDtypeStruct((128, FFL), BF16),
            jax.ShapeDtypeStruct((128, FFL), BF16),
        ),
        in_specs=[any_spec, vmem_spec, any_spec, any_spec, any_spec],
        out_specs=(any_spec, vmem_spec, vmem_spec),
        scratch_shapes=[
            pltpu.VMEM((2, TOK, DL), BF16),
            pltpu.VMEM((2, HALF, DL), BF16),
            pltpu.VMEM((16, FFL, 128), BF16),
            pltpu.VMEM((8, 256, N1), BF16),
            pltpu.VMEM((8, 256, N2), BF16),
            pltpu.VMEM((2, 2, 128, N1), BF16),
            pltpu.VMEM((2, 2, 256, N1), BF16),
            pltpu.VMEM((256, N1), BF16),
            pltpu.VMEM((4, 256, N2), BF16),
            pltpu.VMEM((2, 128, N2), BF16),
            pltpu.VMEM((2, 256, N2), BF16),
            pltpu.VMEM((2, 128, HALF), F32),
            pltpu.VMEM((128, HALF), F32),
            pltpu.VMEM((256, DL), BF16),
            pltpu.VMEM((128, FFL), BF16),
            pltpu.VMEM((128, FFL), BF16),
            pltpu.VMEM((2, 128, DL), F32),
            pltpu.SemaphoreType.DMA((N_COPIES,)),
            pltpu.SemaphoreType.DMA((N_COPIES,)),
            pltpu.SemaphoreType.DMA((4,)),
            pltpu.SemaphoreType.DMA((2,)),
        ],
        compiler_params=pltpu.CompilerParams(
            collective_id=0, has_side_effects=True, vmem_limit_bytes=62 * 2**20
        ),
        cost_estimate=pl.CostEstimate(flops=4 * TOK * FFL * DL, bytes_accessed=24 * 2**20, transcendentals=2 * 128 * FFL),
    )(grad_values, row_scale.reshape(2, 128), gate_input, up_input, down_weight)


def solution(mesh):
    return jax.shard_map(
        body,
        mesh=mesh,
        in_specs=(
            P("tensor", "dp"),
            P("tensor"),
            P("dp", "tensor"),
            P("dp", "tensor"),
            P("tensor", "dp"),
        ),
        out_specs=(P("tensor", "dp"), P("dp", "tensor"), P("dp", "tensor")),
        check_vma=False,
    )
```

```python
import functools

import jax
import jax.numpy as jnp
from jax import lax
from jax.experimental import pallas as pl
from jax.experimental.pallas import tpu as pltpu
from jax.sharding import PartitionSpec as P

MESH = pl.DeviceIdType.MESH
BF16 = jnp.bfloat16
F32 = jnp.float32

TOK = 2048
FFL = 3328
HALF = FFL // 2
DL = 1024
N1 = 1024
N2 = HALF - N1
N_COPIES = 96


def sigmoid(v):
    return 0.5 * jnp.tanh(0.5 * v) + 0.5


class Copies:
    def __init__(self, send_sem, recv_sem):
        self.send_sem, self.recv_sem = send_sem, recv_sem
        self.sent = []

    def send(self, src, dst, device):
        index = len(self.sent)
        copy = pltpu.make_async_remote_copy(
            src_ref=src,
            dst_ref=dst,
            send_sem=self.send_sem.at[index],
            recv_sem=self.recv_sem.at[index],
            device_id=device,
            device_id_type=MESH,
        )
        copy.start()
        self.sent.append(copy)
        return index

    def arrived(self, index):
        self.sent[index].wait_recv()

    def finish(self):
        for copy in self.sent:
            copy.wait_send()


def kernel(
    values, scale, gate, up, weight,
    dg, hg, gate_in, up_in,
    g_all, w_both, h_all, p1, p2, r1a, r1b, r1y, r2y, r2a, r2b, fin, v_in,
    send_sem, recv_sem, load_sem,
):
    dp = lax.axis_index("dp")
    tensor = lax.axis_index("tensor")
    c = lax.rem(dp, 2)
    yh = lax.rem(dp // 2, 2)
    x = dp // 4
    yl = tensor // 4
    z = lax.rem(tensor, 4)
    q = dp // 2

    def wrap(i):
        return lax.rem(i + 4, 4)

    xr, xl, xf = wrap(x + 1), wrap(x - 1), wrap(x + 2)
    zr, zl, zf = wrap(z + 1), wrap(z - 1), wrap(z + 2)
    to_xr = (xr * 4 + yh * 2 + c, tensor)
    to_xl = (xl * 4 + yh * 2 + c, tensor)
    to_yh = (x * 4 + (1 - yh) * 2 + c, tensor)
    to_core = (q * 2 + (1 - c), tensor)
    to_yl = (dp, (1 - yl) * 4 + z)
    to_zr = (dp, yl * 4 + zr)
    to_zl = (dp, yl * 4 + zl)

    def chip(xx, yy):
        return xx * 2 + yy

    def load(i, src, dst):
        copy = pltpu.make_async_copy(src, dst, load_sem.at[i])
        copy.start()
        return copy

    own_half = pl.ds(pl.multiple_of(c * HALF, 128), HALF)
    sib_half = pl.ds(pl.multiple_of((1 - c) * HALF, 128), HALF)
    load_v = load(0, values, v_in)
    load_g = load(1, gate, gate_in)
    load_u = load(2, up, up_in)

    barrier = pltpu.get_barrier_semaphore()
    for neighbour in (to_xr, to_xl, to_yh, to_core, to_yl, to_zr, to_zl):
        pl.semaphore_signal(barrier, inc=1, device_id=neighbour, device_id_type=MESH)
    pl.semaphore_wait(barrier, 7)

    net = Copies(send_sem, recv_sem)
    send, arrived = net.send, net.arrived

    def g_rows(block, first=0, rows=256):
        return g_all.at[c, pl.ds(pl.multiple_of(block * 256 + first, 128), rows)]

    def send_g(block, device, first=0, rows=256):
        ref = g_rows(block, first, rows)
        return send(ref, ref, device)

    load_v.wait()
    own = tensor
    for i in range(2):
        col = jnp.broadcast_to(scale[i : i + 1, :], (128, 128)).T
        for k in range(DL // 128):
            part = v_in[i * 128 : (i + 1) * 128, k * 128 : (k + 1) * 128].astype(F32) * col
            g_all[c, pl.ds(pl.multiple_of(own * 256 + i * 128, 128), 128), k * 128 : (k + 1) * 128] = part.astype(BF16)
    a_yl = send_g(own, to_yl)
    a_zr = send_g(own, to_zr)
    a_zl = send_g(own, to_zl)
    s_own = send_g(own, to_core)

    load_g.wait()
    load_u.wait()

    def hidden(half):
        def tile(k, _):
            cols = pl.ds(pl.multiple_of(half * HALF + k * 128, 128), 128)
            gate_f = gate_in[:, cols].astype(F32)
            h = gate_f * sigmoid(gate_f) * up_in[:, cols].astype(F32)
            h_all[dp, cols, :] = h.T.astype(BF16)
            return 0

        lax.fori_loop(0, HALF // 128, tile, 0, unroll=True)

    base = pl.multiple_of(c * HALF, 128)
    rows1 = pl.ds(base, N1)
    rows2 = pl.ds(pl.multiple_of(base + N1, 128), N2)

    def send_h(first, count, rows, device):
        ref = h_all.at[pl.ds(first, count), rows]
        return send(ref, ref, device)

    hidden(1 - c)
    s_h = send_h(dp, 1, sib_half, to_core)
    hidden(c)
    arrived(s_h)
    b2_xr = send_h(2 * q, 2, rows2, to_xr)
    b2_xl = send_h(2 * q, 2, rows2, to_xl)
    b1_y = send_h(2 * q, 2, rows1, to_yh)
    b1_xr = send_h(2 * q, 2, rows1, to_xr)
    b1_xl = send_h(2 * q, 2, rows1, to_xl)
    b2_y = send_h(2 * q, 2, rows2, to_yh)
    load_w = load(3, weight.at[own_half], w_both.at[c])
    w_sib = send(weight.at[sib_half], w_both.at[c], to_core)

    sib = [send_h(dp, 1, own_half, to_core)]

    def share_h(first, count, rows):
        sib.append(send_h(first, count, rows, to_core))

    def product(block):
        rows = pl.ds(pl.multiple_of(block * 256, 256), 256)

        def cols_of(first, width):
            w_rows = pl.ds(first, width)
            total = lax.dot_general(
                g_all[0, rows, :], w_both[0, w_rows, :], (((1,), (1,)), ((), ())), preferred_element_type=F32
            )
            total += lax.dot_general(
                g_all[1, rows, :], w_both[1, w_rows, :], (((1,), (1,)), ((), ())), preferred_element_type=F32
            )
            return total.astype(BF16)

        def tile(n, _):
            first = pl.multiple_of(n * 256, 256)
            p1[block, :, pl.ds(first, 256)] = cols_of(first, 256)
            return 0

        lax.fori_loop(0, N1 // 256, tile, 0)
        p2[block, :, :] = cols_of(N1, N2)

    ql, qr, qf = chip(xl, yh), chip(xr, yh), chip(xf, yh)
    qy, qyl, qyr, qyf = chip(x, 1 - yh), chip(xl, 1 - yh), chip(xr, 1 - yh), chip(xf, 1 - yh)
    other = (1 - yl) * 4 + z
    ol, orr = (1 - yl) * 4 + zl, (1 - yl) * 4 + zr

    arrived(b2_xr)
    b2_fr = send_h(2 * ql, 1, rows2, to_xr)
    b2_yl = send_h(2 * ql, 2, rows2, to_yh)
    arrived(b2_xl)
    b2_fl = send_h(2 * qr + 1, 1, rows2, to_xl)
    b2_yr = send_h(2 * qr, 2, rows2, to_yh)

    arrived(a_yl)
    a_yzr = send_g(other, to_zr)
    a_yzl = send_g(other, to_zl)
    s_other = send_g(other, to_core)
    arrived(a_zr)
    a_fr = send_g(yl * 4 + zl, to_zr, 0, 128)
    s_zl = send_g(yl * 4 + zl, to_core)
    arrived(a_zl)
    a_fl = send_g(yl * 4 + zr, to_zl, 128, 128)
    s_zr = send_g(yl * 4 + zr, to_core)
    share_h(2 * ql, 2, rows2)
    share_h(2 * qr, 2, rows2)

    load_w.wait()
    arrived(w_sib)
    arrived(s_own)
    arrived(s_other)

    def near(i, _):
        product(i * 4 + z)
        return 0

    lax.fori_loop(0, 2, near, 0)

    arrived(b1_xr)
    b1_fr = send_h(2 * ql, 1, rows1, to_xr)
    arrived(b1_xl)
    b1_fl = send_h(2 * qr + 1, 1, rows1, to_xl)

    arrived(a_yzr)
    a_yfr = send_g(ol, to_zr, 0, 128)
    s_ol = send_g(ol, to_core)
    arrived(a_yzl)
    a_yfl = send_g(orr, to_zl, 128, 128)
    s_or = send_g(orr, to_core)

    arrived(b1_y)
    b1_yxr = send_h(2 * qy, 2, rows1, to_xr)
    b1_yxl = send_h(2 * qy, 2, rows1, to_xl)
    share_h(2 * ql, 2, rows1)
    share_h(2 * qr, 2, rows1)
    share_h(2 * qy, 2, rows1)

    arrived(b2_fr)
    arrived(b2_fl)
    b2_yf = send_h(2 * qf, 2, rows2, to_yh)
    share_h(2 * qf, 2, rows2)

    for s in (s_zl, s_zr, s_ol, s_or):
        arrived(s)

    def middle(i, _):
        product((i // 2) * 4 + wrap(z - 1 + 2 * lax.rem(i, 2)))
        return 0

    lax.fori_loop(0, 4, middle, 0)

    arrived(a_fr)
    arrived(a_fl)
    s_f = send_g(yl * 4 + zf, to_core)
    arrived(a_yfr)
    arrived(a_yfl)
    s_of = send_g((1 - yl) * 4 + zf, to_core)

    arrived(b1_yxr)
    b1_yfr = send_h(2 * qyl, 1, rows1, to_xr)
    arrived(b1_yxl)
    b1_yfl = send_h(2 * qyr + 1, 1, rows1, to_xl)

    arrived(s_f)
    arrived(s_of)

    def far(i, _):
        product(i * 4 + zf)
        return 0

    lax.fori_loop(0, 2, far, 0)

    top, low = pl.ds(0, 128), pl.ds(128, 128)
    c1 = [[], []]

    def step1(place, yy):
        block = chip(xf, yy)
        return (
            send(p1.at[block, top], r1a.at[0, place], to_xr),
            send(p1.at[block, low], r1a.at[1, place], to_xl),
        )

    def step2_ready(place, yy):
        c1[place].append(send(p1.at[chip(xr, yy), low], r1b.at[0, place, low], to_xr))
        c1[place].append(send(p1.at[chip(xl, yy), top], r1b.at[1, place, top], to_xl))

    def add(dst, rows, others):
        def strip(i, _):
            at = pl.ds(pl.multiple_of(rows[0] + i * 16, 16), 16)
            total = dst[at, :].astype(F32)
            for other_ref, shift in others:
                total += other_ref[pl.ds(pl.multiple_of(rows[0] - shift + i * 16, 16), 16), :].astype(F32)
            dst[at, :] = total.astype(BF16)
            return 0

        lax.fori_loop(0, rows[1] // 16, strip, 0, unroll=2)

    def step2_rest(place, yy, first):
        arrived(first[0])
        add(p1.at[chip(xr, yy)], (0, 128), [(r1a.at[0, place], 0)])
        c1[place].append(send(p1.at[chip(xr, yy), top], r1b.at[0, place, top], to_xr))
        arrived(first[1])
        add(p1.at[chip(xl, yy)], (128, 128), [(r1a.at[1, place], 128)])
        c1[place].append(send(p1.at[chip(xl, yy), low], r1b.at[1, place, low], to_xl))

    first0 = step1(0, 1 - yh)
    c2y_f = send(p2.at[chip(xf, 1 - yh)], r2y.at[xf], to_yh)
    step2_ready(0, 1 - yh)
    c2y_r = send(p2.at[chip(xr, 1 - yh)], r2y.at[xr], to_yh)
    c2y_l = send(p2.at[chip(xl, 1 - yh)], r2y.at[xl], to_yh)
    first1 = step1(1, yh)
    c2y_o = send(p2.at[chip(x, 1 - yh)], r2y.at[x], to_yh)

    arrived(b1_fr)
    arrived(b1_fl)
    share_h(2 * qf, 2, rows1)
    arrived(b2_y)
    share_h(2 * qy, 2, rows2)
    arrived(b2_yl)
    share_h(2 * qyl, 2, rows2)
    arrived(b2_yr)
    share_h(2 * qyr, 2, rows2)
    share_h(2 * qyl, 2, rows1)
    share_h(2 * qyr, 2, rows1)
    arrived(b1_yfr)
    arrived(b1_yfl)
    share_h(2 * qyf, 2, rows1)
    arrived(b2_yf)
    share_h(2 * qyf, 2, rows2)

    step2_rest(0, 1 - yh, first0)
    step2_ready(1, yh)

    def dg_tile(m, _):
        rows = pl.ds(pl.multiple_of(m * 128, 128), 128)
        lhs = jnp.concatenate([h_all[s, rows, :] for s in range(16)], axis=1)
        dg[rows, :] = jnp.dot(lhs, g_all[c], preferred_element_type=F32).astype(BF16)
        return 0

    def down(first, last):
        lax.fori_loop(first, last, dg_tile, 0)

    for s in sib:
        arrived(s)
    arrived(c2y_f)
    bf = chip(xf, yh)
    add(p2.at[bf], (0, 256), [(r2y.at[xf], 0)])
    c2a_r = send(p2.at[bf, top], r2a.at[0], to_xr)
    c2a_l = send(p2.at[bf, low], r2a.at[1], to_xl)
    down(0, 4)
    step2_rest(1, yh, first1)
    down(4, 9)
    for s in c1[0]:
        arrived(s)
    bo = chip(x, 1 - yh)
    add(p1.at[bo], (0, 256), [(r1b.at[0, 0], 0), (r1b.at[1, 0], 0)])
    c1_y = send(p1.at[bo], r1y, to_yh)
    br, bl = chip(xr, yh), chip(xl, yh)
    arrived(c2y_r)
    add(p2.at[br], (128, 128), [(r2y.at[xr], 0)])
    c2_r = [send(p2.at[br, low], r2b.at[0, low], to_xr)]
    arrived(c2y_l)
    add(p2.at[bl], (0, 128), [(r2y.at[xl], 0)])
    c2_l = [send(p2.at[bl, top], r2b.at[1, top], to_xl)]
    down(9, 12)
    arrived(c2a_r)
    add(p2.at[br], (0, 128), [(r2y.at[xr], 0), (r2a.at[0], 0)])
    c2_r.append(send(p2.at[br, top], r2b.at[0, top], to_xr))
    arrived(c2a_l)
    add(p2.at[bl], (128, 128), [(r2y.at[xl], 0), (r2a.at[1], 128)])
    c2_l.append(send(p2.at[bl, low], r2b.at[1, low], to_xl))
    down(12, 26)

    own_rows = pl.multiple_of(c * 128, 128)
    sib_rows = pl.multiple_of((1 - c) * 128, 128)

    def total_of(first, dst, cols, terms):
        def strip(i, _):
            at = pl.ds(pl.multiple_of(first + i * 16, 16), 16)
            total = terms[0][at, :].astype(F32)
            for term in terms[1:]:
                total += term[at, :].astype(F32)
            dst[pl.ds(pl.multiple_of(i * 16, 16), 16), cols] = total
            return 0

        lax.fori_loop(0, 8, strip, 0)

    terms2 = [p2.at[q], r2y.at[x], r2b.at[0], r2b.at[1]]
    terms1 = [p1.at[q], r1b.at[0, 1], r1b.at[1, 1], r1y]
    cols1, cols2 = slice(0, N1), slice(N1, HALF)
    for s in c1[1]:
        arrived(s)
    arrived(c1_y)
    total_of(sib_rows, fin, cols1, terms1)
    last1 = send(fin.at[:, cols1], hg.at[c, :, cols1], to_core)
    total_of(own_rows, hg.at[c], cols1, terms1)
    for s in c2_r + c2_l + [c2y_o]:
        arrived(s)
    total_of(sib_rows, fin, cols2, terms2)
    last2 = send(fin.at[:, cols2], hg.at[c, :, cols2], to_core)
    total_of(own_rows, hg.at[c], cols2, terms2)
    arrived(last1)
    arrived(last2)
    net.finish()


BANDS = 13


def writer(dg, hg, gate, up, dg_out, gg_out, ug_out, buf, gg, ug, buf_sem, out_sem):
    rows = FFL // BANDS

    def band(k):
        slot = k % 4
        return pltpu.make_async_copy(buf.at[slot], dg_out.at[pl.ds(k * rows, rows)], buf_sem.at[slot])

    def finish(half):
        for k in range(HALF // 128):
            cols = slice(half * HALF + k * 128, half * HALF + (k + 1) * 128)
            grad = hg[half, :, k * 128 : (k + 1) * 128]
            gate_f = gate[:, cols].astype(F32)
            s = sigmoid(gate_f)
            gg[:, cols] = (grad * up[:, cols].astype(F32) * s * (1.0 + gate_f * (1.0 - s))).astype(BF16)
            ug[:, cols] = (grad * (gate_f * s)).astype(BF16)

    for k in range(BANDS):
        if k >= 4:
            band(k - 4).wait()
        buf[k % 4] = dg[k * rows : (k + 1) * rows, :].astype(F32)
        band(k).start()
        if k == 3:
            finish(0)
        if k == 7:
            finish(1)
            outs = [
                pltpu.make_async_copy(gg, gg_out, out_sem.at[0]),
                pltpu.make_async_copy(ug, ug_out, out_sem.at[1]),
            ]
            for out in outs:
                out.start()
    for k in range(BANDS - 4, BANDS):
        band(k).wait()
    for out in outs:
        out.wait()


def body(grad_values, row_scale, gate_input, up_input, down_weight):
    any_spec = pl.BlockSpec(memory_space=pl.ANY)
    vmem_spec = pl.BlockSpec(memory_space=pltpu.VMEM)
    held = pl.pallas_call(
        kernel,
        out_shape=(
            pltpu.VMEM((FFL, DL), BF16),
            pltpu.VMEM((2, 128, HALF), F32),
            pltpu.VMEM((128, FFL), BF16),
            pltpu.VMEM((128, FFL), BF16),
        ),
        in_specs=[any_spec, vmem_spec, any_spec, any_spec, any_spec],
        out_specs=(vmem_spec,) * 4,
        scratch_shapes=[
            pltpu.VMEM((2, TOK, DL), BF16),
            pltpu.VMEM((2, HALF, DL), BF16),
            pltpu.VMEM((16, FFL, 128), BF16),
            pltpu.VMEM((8, 256, N1), BF16),
            pltpu.VMEM((8, 256, N2), BF16),
            pltpu.VMEM((2, 2, 128, N1), BF16),
            pltpu.VMEM((2, 2, 256, N1), BF16),
            pltpu.VMEM((256, N1), BF16),
            pltpu.VMEM((4, 256, N2), BF16),
            pltpu.VMEM((2, 128, N2), BF16),
            pltpu.VMEM((2, 256, N2), BF16),
            pltpu.VMEM((128, HALF), F32),
            pltpu.VMEM((256, DL), BF16),
            pltpu.SemaphoreType.DMA((N_COPIES,)),
            pltpu.SemaphoreType.DMA((N_COPIES,)),
            pltpu.SemaphoreType.DMA((4,)),
        ],
        compiler_params=pltpu.CompilerParams(
            collective_id=0, has_side_effects=True, vmem_limit_bytes=48 * 2**20
        ),
        cost_estimate=pl.CostEstimate(flops=4 * TOK * FFL * DL, bytes_accessed=24 * 2**20, transcendentals=128 * FFL),
    )(grad_values, row_scale.reshape(2, 128), gate_input, up_input, down_weight)
    return pl.pallas_call(
        writer,
        out_shape=(
            jax.ShapeDtypeStruct((FFL, DL), F32),
            jax.ShapeDtypeStruct((128, FFL), BF16),
            jax.ShapeDtypeStruct((128, FFL), BF16),
        ),
        in_specs=[vmem_spec] * 4,
        out_specs=(any_spec,) * 3,
        scratch_shapes=[
            pltpu.VMEM((4, FFL // BANDS, DL), F32),
            pltpu.VMEM((128, FFL), BF16),
            pltpu.VMEM((128, FFL), BF16),
            pltpu.SemaphoreType.DMA((4,)),
            pltpu.SemaphoreType.DMA((2,)),
        ],
        compiler_params=pltpu.CompilerParams(vmem_limit_bytes=16 * 2**20),
        cost_estimate=pl.CostEstimate(flops=20 * 128 * FFL, bytes_accessed=24 * 2**20, transcendentals=128 * FFL),
    )(*held)


def solution(mesh):
    return jax.shard_map(
        body,
        mesh=mesh,
        in_specs=(
            P("tensor", "dp"),
            P("tensor"),
            P("dp", "tensor"),
            P("dp", "tensor"),
            P("tensor", "dp"),
        ),
        out_specs=(P("tensor", "dp"), P("dp", "tensor"), P("dp", "tensor")),
        check_vma=False,
    )
```

```python
import functools

import jax
import jax.numpy as jnp
from jax import lax
from jax.experimental import pallas as pl
from jax.experimental.pallas import tpu as pltpu
from jax.sharding import PartitionSpec as P

MESH = pl.DeviceIdType.MESH
BF16 = jnp.bfloat16
F32 = jnp.float32

TOK = 2048
FFL = 3328
HALF = FFL // 2
DL = 1024
N1 = 1024
N2 = HALF - N1
B1 = 1024
B2 = HALF - B1
N_COPIES = 128


def sigmoid(v):
    return 0.5 * jnp.tanh(0.5 * v) + 0.5


class Copies:
    def __init__(self, send_sem, recv_sem):
        self.send_sem, self.recv_sem = send_sem, recv_sem
        self.sent = []

    def send(self, src, dst, device):
        index = len(self.sent)
        copy = pltpu.make_async_remote_copy(
            src_ref=src,
            dst_ref=dst,
            send_sem=self.send_sem.at[index],
            recv_sem=self.recv_sem.at[index],
            device_id=device,
            device_id_type=MESH,
        )
        copy.start()
        self.sent.append(copy)
        return index

    def arrived(self, index):
        self.sent[index].wait_recv()

    def finish(self):
        for copy in self.sent:
            copy.wait_send()


def kernel(
    values, scale, gate, up, weight,
    dg, hg, gate_in, up_in,
    g_all, w_both, h_all, p1, p2, r1a, r1b, r1y, r2y, r2a, r2b, fin, v_in,
    send_sem, recv_sem, load_sem,
):
    dp = lax.axis_index("dp")
    tensor = lax.axis_index("tensor")
    c = lax.rem(dp, 2)
    yh = lax.rem(dp // 2, 2)
    x = dp // 4
    yl = tensor // 4
    z = lax.rem(tensor, 4)
    q = dp // 2

    def wrap(i):
        return lax.rem(i + 4, 4)

    xr, xl, xf = wrap(x + 1), wrap(x - 1), wrap(x + 2)
    zr, zl, zf = wrap(z + 1), wrap(z - 1), wrap(z + 2)
    to_xr = (xr * 4 + yh * 2 + c, tensor)
    to_xl = (xl * 4 + yh * 2 + c, tensor)
    to_yh = (x * 4 + (1 - yh) * 2 + c, tensor)
    to_core = (q * 2 + (1 - c), tensor)
    to_yl = (dp, (1 - yl) * 4 + z)
    to_zr = (dp, yl * 4 + zr)
    to_zl = (dp, yl * 4 + zl)

    def chip(xx, yy):
        return xx * 2 + yy

    def load(i, src, dst):
        copy = pltpu.make_async_copy(src, dst, load_sem.at[i])
        copy.start()
        return copy

    own_half = pl.ds(pl.multiple_of(c * HALF, 128), HALF)
    sib_half = pl.ds(pl.multiple_of((1 - c) * HALF, 128), HALF)
    load_v = load(0, values, v_in)
    load_g = load(1, gate, gate_in)
    load_u = load(2, up, up_in)

    barrier = pltpu.get_barrier_semaphore()
    for neighbour in (to_xr, to_xl, to_yh, to_core, to_yl, to_zr, to_zl):
        pl.semaphore_signal(barrier, inc=1, device_id=neighbour, device_id_type=MESH)
    pl.semaphore_wait(barrier, 7)

    net = Copies(send_sem, recv_sem)
    send, arrived = net.send, net.arrived

    def g_rows(block, first=0, rows=256):
        return g_all.at[c, pl.ds(pl.multiple_of(block * 256 + first, 128), rows)]

    def send_g(block, device, first=0, rows=256):
        ref = g_rows(block, first, rows)
        return send(ref, ref, device)

    load_v.wait()
    own = tensor
    for i in range(2):
        col = jnp.broadcast_to(scale[i : i + 1, :], (128, 128)).T
        for k in range(DL // 128):
            part = v_in[i * 128 : (i + 1) * 128, k * 128 : (k + 1) * 128].astype(F32) * col
            g_all[c, pl.ds(pl.multiple_of(own * 256 + i * 128, 128), 128), k * 128 : (k + 1) * 128] = part.astype(BF16)
    a_yl = send_g(own, to_yl)
    a_zr = send_g(own, to_zr)
    a_zl = send_g(own, to_zl)
    s_own = send_g(own, to_core)

    load_g.wait()
    load_u.wait()

    def hidden(half, first, last):
        def tile(k, _):
            cols = pl.ds(pl.multiple_of(half * HALF + k * 128, 128), 128)
            gate_f = gate_in[:, cols].astype(F32)
            h = gate_f * sigmoid(gate_f) * up_in[:, cols].astype(F32)
            h_all[dp, cols, :] = h.T.astype(BF16)
            return 0

        lax.fori_loop(first, last, tile, 0, unroll=True)

    def h_rows(half, first, count):
        return pl.ds(pl.multiple_of(half * HALF + first, 16), count)

    rows1 = h_rows(c, 0, B1)
    rows1a, rows1b = h_rows(c, 0, B1 // 2), h_rows(c, B1 // 2, B1 // 2)
    rows2 = h_rows(c, B1, B2)

    def send_h(first, count, rows, device):
        ref = h_all.at[pl.ds(first, count), rows]
        return send(ref, ref, device)

    twin = 2 * q + 1 - c
    edge = B1 // 128
    hidden(c, edge, HALF // 128)
    b2_xr = [send_h(dp, 1, rows2, to_xr)]
    b2_xl = [send_h(dp, 1, rows2, to_xl)]
    hidden(1 - c, edge, HALF // 128)
    s_h2 = send_h(dp, 1, h_rows(1 - c, B1, B2), to_core)
    hidden(c, 0, edge)
    b1_y = [send_h(dp, 1, rows1, to_yh)]
    b1_xr = [send_h(dp, 1, rows1, to_xr)]
    b1_xl = [send_h(dp, 1, rows1, to_xl)]
    hidden(1 - c, 0, edge)
    s_h1 = send_h(dp, 1, h_rows(1 - c, 0, B1), to_core)
    arrived(s_h2)
    b2_xr.append(send_h(twin, 1, rows2, to_xr))
    b2_xl.append(send_h(twin, 1, rows2, to_xl))
    arrived(s_h1)
    b1_y.append(send_h(twin, 1, rows1, to_yh))
    b1_xr.append(send_h(twin, 1, rows1, to_xr))
    b1_xl.append(send_h(twin, 1, rows1, to_xl))
    b2_y = send_h(2 * q, 2, rows2, to_yh)
    load_w = load(3, weight.at[own_half], w_both.at[c])
    w_sib = send(weight.at[sib_half], w_both.at[c], to_core)

    sib = [send_h(dp, 1, own_half, to_core)]

    def share_h(first, count, rows):
        sib.append(send_h(first, count, rows, to_core))

    def product(block):
        rows = pl.ds(pl.multiple_of(block * 256, 256), 256)

        def cols_of(first, width):
            w_rows = pl.ds(first, width)
            total = lax.dot_general(
                g_all[0, rows, :], w_both[0, w_rows, :], (((1,), (1,)), ((), ())), preferred_element_type=F32
            )
            total += lax.dot_general(
                g_all[1, rows, :], w_both[1, w_rows, :], (((1,), (1,)), ((), ())), preferred_element_type=F32
            )
            return total.astype(BF16)

        for first in range(0, N1, 512):
            p1[block, :, first : first + 512] = cols_of(first, 512)
        p2[block, :, :] = cols_of(N1, N2)

    ql, qr, qf = chip(xl, yh), chip(xr, yh), chip(xf, yh)
    qy, qyl, qyr, qyf = chip(x, 1 - yh), chip(xl, 1 - yh), chip(xr, 1 - yh), chip(xf, 1 - yh)
    other = (1 - yl) * 4 + z
    ol, orr = (1 - yl) * 4 + zl, (1 - yl) * 4 + zr

    for s in b2_xr:
        arrived(s)
    b2_fr = send_h(2 * ql + c, 1, rows2, to_xr)
    b2_yl = send_h(2 * ql, 2, rows2, to_yh)
    for s in b2_xl:
        arrived(s)
    b2_fl = send_h(2 * qr + 1 - c, 1, rows2, to_xl)
    b2_yr = send_h(2 * qr, 2, rows2, to_yh)

    arrived(a_yl)
    a_yzr = send_g(other, to_zr)
    a_yzl = send_g(other, to_zl)
    s_other = send_g(other, to_core)
    arrived(a_zr)
    a_fr = send_g(yl * 4 + zl, to_zr, 0, 128)
    s_zl = send_g(yl * 4 + zl, to_core)
    arrived(a_zl)
    a_fl = send_g(yl * 4 + zr, to_zl, 128, 128)
    s_zr = send_g(yl * 4 + zr, to_core)
    share_h(2 * ql, 2, rows2)
    share_h(2 * qr, 2, rows2)

    load_w.wait()
    arrived(w_sib)
    arrived(s_own)
    arrived(s_other)

    def near(i, _):
        product(i * 4 + z)
        return 0

    lax.fori_loop(0, 2, near, 0)

    for s in b1_xr:
        arrived(s)
    b1_fr = [send_h(2 * ql + c, 1, rows1a, to_xr)]
    for s in b1_xl:
        arrived(s)
    b1_fl = [send_h(2 * qr + 1 - c, 1, rows1a, to_xl)]

    arrived(a_yzr)
    a_yfr = send_g(ol, to_zr, 0, 128)
    s_ol = send_g(ol, to_core)
    arrived(a_yzl)
    a_yfl = send_g(orr, to_zl, 128, 128)
    s_or = send_g(orr, to_core)

    for s in b1_y:
        arrived(s)
    b1_yxr = send_h(2 * qy, 2, rows1, to_xr)
    b1_yxl = send_h(2 * qy, 2, rows1, to_xl)
    b1_fr.append(send_h(2 * ql + c, 1, rows1b, to_xr))
    b1_fl.append(send_h(2 * qr + 1 - c, 1, rows1b, to_xl))
    share_h(2 * ql, 2, rows1)
    share_h(2 * qr, 2, rows1)
    share_h(2 * qy, 2, rows1)

    arrived(b2_fr)
    arrived(b2_fl)
    b2_yf = send_h(2 * qf, 2, rows2, to_yh)
    share_h(2 * qf, 2, rows2)

    for s in (s_zl, s_zr, s_ol, s_or):
        arrived(s)

    def middle(i, _):
        product((i // 2) * 4 + wrap(z - 1 + 2 * lax.rem(i, 2)))
        return 0

    lax.fori_loop(0, 4, middle, 0)

    arrived(a_fr)
    arrived(a_fl)
    s_f = send_g(yl * 4 + zf, to_core)
    arrived(a_yfr)
    arrived(a_yfl)
    s_of = send_g((1 - yl) * 4 + zf, to_core)

    arrived(b1_yxr)
    b1_yfr = send_h(2 * qyl, 1, rows1, to_xr)
    arrived(b1_yxl)
    b1_yfl = send_h(2 * qyr + 1, 1, rows1, to_xl)

    arrived(s_f)
    arrived(s_of)

    def far(i, _):
        product(i * 4 + zf)
        return 0

    lax.fori_loop(0, 2, far, 0)

    top, low = pl.ds(0, 128), pl.ds(128, 128)
    c1 = [[], []]

    def step1(place, yy):
        block = chip(xf, yy)
        return (
            send(p1.at[block, top], r1a.at[0, place], to_xr),
            send(p1.at[block, low], r1a.at[1, place], to_xl),
        )

    def step2_ready(place, yy):
        c1[place].append(send(p1.at[chip(xr, yy), low], r1b.at[0, place, low], to_xr))
        c1[place].append(send(p1.at[chip(xl, yy), top], r1b.at[1, place, top], to_xl))

    def add(dst, rows, others):
        def strip(i, _):
            at = pl.ds(pl.multiple_of(rows[0] + i * 16, 16), 16)
            total = dst[at, :].astype(F32)
            for other_ref, shift in others:
                total += other_ref[pl.ds(pl.multiple_of(rows[0] - shift + i * 16, 16), 16), :].astype(F32)
            dst[at, :] = total.astype(BF16)
            return 0

        lax.fori_loop(0, rows[1] // 16, strip, 0, unroll=2)

    def step2_rest(place, yy, first):
        arrived(first[0])
        add(p1.at[chip(xr, yy)], (0, 128), [(r1a.at[0, place], 0)])
        c1[place].append(send(p1.at[chip(xr, yy), top], r1b.at[0, place, top], to_xr))
        arrived(first[1])
        add(p1.at[chip(xl, yy)], (128, 128), [(r1a.at[1, place], 128)])
        c1[place].append(send(p1.at[chip(xl, yy), low], r1b.at[1, place, low], to_xl))

    first0 = step1(0, 1 - yh)
    c2y_f = send(p2.at[chip(xf, 1 - yh)], r2y.at[xf], to_yh)
    step2_ready(0, 1 - yh)
    c2y_r = send(p2.at[chip(xr, 1 - yh)], r2y.at[xr], to_yh)
    c2y_l = send(p2.at[chip(xl, 1 - yh)], r2y.at[xl], to_yh)
    first1 = step1(1, yh)
    c2y_o = send(p2.at[chip(x, 1 - yh)], r2y.at[x], to_yh)

    for s in b1_fr + b1_fl:
        arrived(s)
    share_h(2 * qf, 2, rows1)
    arrived(b2_y)
    share_h(2 * qy, 2, rows2)
    arrived(b2_yl)
    share_h(2 * qyl, 2, rows2)
    arrived(b2_yr)
    share_h(2 * qyr, 2, rows2)
    share_h(2 * qyl, 2, rows1)
    share_h(2 * qyr, 2, rows1)
    arrived(b1_yfr)
    arrived(b1_yfl)
    share_h(2 * qyf, 2, rows1)
    arrived(b2_yf)
    share_h(2 * qyf, 2, rows2)

    step2_rest(0, 1 - yh, first0)
    step2_ready(1, yh)

    def dg_tile(m, _):
        rows = pl.ds(pl.multiple_of(m * 256, 256), 256)
        lhs = jnp.concatenate([h_all[s, rows, :] for s in range(16)], axis=1)
        dg[rows, :] = jnp.dot(lhs, g_all[c], preferred_element_type=F32).astype(BF16)
        return 0

    def down(first, last):
        lax.fori_loop(first, last, dg_tile, 0)

    for s in sib:
        arrived(s)
    arrived(c2y_f)
    bf = chip(xf, yh)
    add(p2.at[bf], (0, 256), [(r2y.at[xf], 0)])
    c2a_r = send(p2.at[bf, top], r2a.at[0], to_xr)
    c2a_l = send(p2.at[bf, low], r2a.at[1], to_xl)
    down(0, 2)
    step2_rest(1, yh, first1)
    down(2, 5)
    for s in c1[0]:
        arrived(s)
    own_rows = pl.multiple_of(c * 128, 128)
    sib_rows = pl.multiple_of((1 - c) * 128, 128)
    bo = chip(x, 1 - yh)
    add(p1.at[bo], (sib_rows, 128), [(r1b.at[0, 0], 0), (r1b.at[1, 0], 0)])
    c1_ys = send(p1.at[bo, pl.ds(sib_rows, 128)], r1y.at[pl.ds(sib_rows, 128)], to_yh)
    add(p1.at[bo], (own_rows, 128), [(r1b.at[0, 0], 0), (r1b.at[1, 0], 0)])
    c1_yo = send(p1.at[bo, pl.ds(own_rows, 128)], r1y.at[pl.ds(own_rows, 128)], to_yh)
    br, bl = chip(xr, yh), chip(xl, yh)
    arrived(c2y_r)
    add(p2.at[br], (128, 128), [(r2y.at[xr], 0)])
    c2_r = [send(p2.at[br, low], r2b.at[0, low], to_xr)]
    down(5, 8)
    arrived(c2y_l)
    add(p2.at[bl], (0, 128), [(r2y.at[xl], 0)])
    c2_l = [send(p2.at[bl, top], r2b.at[1, top], to_xl)]
    down(8, 10)
    arrived(c2a_r)
    add(p2.at[br], (0, 128), [(r2y.at[xr], 0), (r2a.at[0], 0)])
    c2_r.append(send(p2.at[br, top], r2b.at[0, top], to_xr))
    arrived(c2a_l)
    add(p2.at[bl], (128, 128), [(r2y.at[xl], 0), (r2a.at[1], 128)])
    c2_l.append(send(p2.at[bl, low], r2b.at[1, low], to_xl))
    down(10, 13)


    def total_of(first, dst, cols, terms):
        def strip(i, _):
            at = pl.ds(pl.multiple_of(first + i * 16, 16), 16)
            total = terms[0][at, :].astype(F32)
            for term in terms[1:]:
                total += term[at, :].astype(F32)
            dst[pl.ds(pl.multiple_of(i * 16, 16), 16), cols] = total
            return 0

        lax.fori_loop(0, 8, strip, 0)

    terms2 = [p2.at[q], r2y.at[x], r2b.at[0], r2b.at[1]]
    terms1 = [p1.at[q], r1b.at[0, 1], r1b.at[1, 1], r1y]
    cols1, cols2 = slice(0, N1), slice(N1, HALF)
    for s in c1[1] + [c2y_o]:
        arrived(s)
    arrived(c1_ys)
    total_of(sib_rows, fin, cols1, terms1)
    last1 = send(fin.at[:, cols1], hg.at[c, :, cols1], to_core)
    for s in c2_r + c2_l:
        arrived(s)
    total_of(sib_rows, fin, cols2, terms2)
    last2 = send(fin.at[:, cols2], hg.at[c, :, cols2], to_core)
    total_of(own_rows, hg.at[c], cols2, terms2)
    arrived(c1_yo)
    total_of(own_rows, hg.at[c], cols1, terms1)
    arrived(last1)
    arrived(last2)
    net.finish()


BANDS = 13


def writer(dg, hg, gate, up, dg_out, gg_out, ug_out, buf, gg, ug, buf_sem, out_sem):
    rows = FFL // BANDS

    def band(k):
        slot = k % 4
        return pltpu.make_async_copy(buf.at[slot], dg_out.at[pl.ds(k * rows, rows)], buf_sem.at[slot])

    def finish(half):
        for k in range(HALF // 128):
            cols = slice(half * HALF + k * 128, half * HALF + (k + 1) * 128)
            grad = hg[half, :, k * 128 : (k + 1) * 128]
            gate_f = gate[:, cols].astype(F32)
            s = sigmoid(gate_f)
            gg[:, cols] = (grad * up[:, cols].astype(F32) * s * (1.0 + gate_f * (1.0 - s))).astype(BF16)
            ug[:, cols] = (grad * (gate_f * s)).astype(BF16)

    for k in range(BANDS):
        if k >= 4:
            band(k - 4).wait()
        buf[k % 4] = dg[k * rows : (k + 1) * rows, :].astype(F32)
        band(k).start()
        if k == 3:
            finish(0)
        if k == 7:
            finish(1)
            outs = [
                pltpu.make_async_copy(gg, gg_out, out_sem.at[0]),
                pltpu.make_async_copy(ug, ug_out, out_sem.at[1]),
            ]
            for out in outs:
                out.start()
    for k in range(BANDS - 4, BANDS):
        band(k).wait()
    for out in outs:
        out.wait()


def body(grad_values, row_scale, gate_input, up_input, down_weight):
    any_spec = pl.BlockSpec(memory_space=pl.ANY)
    vmem_spec = pl.BlockSpec(memory_space=pltpu.VMEM)
    held = pl.pallas_call(
        kernel,
        out_shape=(
            pltpu.VMEM((FFL, DL), BF16),
            pltpu.VMEM((2, 128, HALF), F32),
            pltpu.VMEM((128, FFL), BF16),
            pltpu.VMEM((128, FFL), BF16),
        ),
        in_specs=[any_spec, vmem_spec, any_spec, any_spec, any_spec],
        out_specs=(vmem_spec,) * 4,
        scratch_shapes=[
            pltpu.VMEM((2, TOK, DL), BF16),
            pltpu.VMEM((2, HALF, DL), BF16),
            pltpu.VMEM((16, FFL, 128), BF16),
            pltpu.VMEM((8, 256, N1), BF16),
            pltpu.VMEM((8, 256, N2), BF16),
            pltpu.VMEM((2, 2, 128, N1), BF16),
            pltpu.VMEM((2, 2, 256, N1), BF16),
            pltpu.VMEM((256, N1), BF16),
            pltpu.VMEM((4, 256, N2), BF16),
            pltpu.VMEM((2, 128, N2), BF16),
            pltpu.VMEM((2, 256, N2), BF16),
            pltpu.VMEM((128, HALF), F32),
            pltpu.VMEM((256, DL), BF16),
            pltpu.SemaphoreType.DMA((N_COPIES,)),
            pltpu.SemaphoreType.DMA((N_COPIES,)),
            pltpu.SemaphoreType.DMA((4,)),
        ],
        compiler_params=pltpu.CompilerParams(
            collective_id=0, has_side_effects=True, vmem_limit_bytes=48 * 2**20
        ),
        cost_estimate=pl.CostEstimate(flops=4 * TOK * FFL * DL, bytes_accessed=24 * 2**20, transcendentals=128 * FFL),
    )(grad_values, row_scale.reshape(2, 128), gate_input, up_input, down_weight)
    return pl.pallas_call(
        writer,
        out_shape=(
            jax.ShapeDtypeStruct((FFL, DL), F32),
            jax.ShapeDtypeStruct((128, FFL), BF16),
            jax.ShapeDtypeStruct((128, FFL), BF16),
        ),
        in_specs=[vmem_spec] * 4,
        out_specs=(any_spec,) * 3,
        scratch_shapes=[
            pltpu.VMEM((4, FFL // BANDS, DL), F32),
            pltpu.VMEM((128, FFL), BF16),
            pltpu.VMEM((128, FFL), BF16),
            pltpu.SemaphoreType.DMA((4,)),
            pltpu.SemaphoreType.DMA((2,)),
        ],
        compiler_params=pltpu.CompilerParams(vmem_limit_bytes=16 * 2**20),
        cost_estimate=pl.CostEstimate(flops=20 * 128 * FFL, bytes_accessed=24 * 2**20, transcendentals=128 * FFL),
    )(*held)


def solution(mesh):
    return jax.shard_map(
        body,
        mesh=mesh,
        in_specs=(
            P("tensor", "dp"),
            P("tensor"),
            P("dp", "tensor"),
            P("dp", "tensor"),
            P("tensor", "dp"),
        ),
        out_specs=(P("tensor", "dp"), P("dp", "tensor"), P("dp", "tensor")),
        check_vma=False,
    )
```

```python
import functools

import jax
import jax.numpy as jnp
from jax import lax
from jax.experimental import pallas as pl
from jax.experimental.pallas import tpu as pltpu
from jax.sharding import PartitionSpec as P

MESH = pl.DeviceIdType.MESH
BF16 = jnp.bfloat16
F32 = jnp.float32

TOK = 2048
FFL = 3328
HALF = FFL // 2
DL = 1024
N1 = 1024
N2 = HALF - N1
B1 = 1024
B2 = HALF - B1
N_COPIES = 128


def sigmoid(v):
    return 0.5 * jnp.tanh(0.5 * v) + 0.5


class Copies:
    def __init__(self, send_sem, recv_sem):
        self.send_sem, self.recv_sem = send_sem, recv_sem
        self.sent = []

    def send(self, src, dst, device):
        index = len(self.sent)
        copy = pltpu.make_async_remote_copy(
            src_ref=src,
            dst_ref=dst,
            send_sem=self.send_sem.at[index],
            recv_sem=self.recv_sem.at[index],
            device_id=device,
            device_id_type=MESH,
        )
        copy.start()
        self.sent.append(copy)
        return index

    def arrived(self, index):
        self.sent[index].wait_recv()

    def finish(self):
        for copy in self.sent:
            copy.wait_send()


def kernel(
    values, scale, gate, up, weight,
    dg, s1, s2, gate_in, up_in,
    g_all, w_both, h_all, p1, p2, r1a, r1b, r2y, r2a, v_in, scale_in,
    send_sem, recv_sem, load_sem,
):
    dp = lax.axis_index("dp")
    tensor = lax.axis_index("tensor")
    c = lax.rem(dp, 2)
    yh = lax.rem(dp // 2, 2)
    x = dp // 4
    yl = tensor // 4
    z = lax.rem(tensor, 4)
    q = dp // 2

    def wrap(i):
        return lax.rem(i + 4, 4)

    xr, xl, xf = wrap(x + 1), wrap(x - 1), wrap(x + 2)
    zr, zl, zf = wrap(z + 1), wrap(z - 1), wrap(z + 2)
    to_xr = (xr * 4 + yh * 2 + c, tensor)
    to_xl = (xl * 4 + yh * 2 + c, tensor)
    to_yh = (x * 4 + (1 - yh) * 2 + c, tensor)
    to_xr_twin = (xr * 4 + yh * 2 + 1 - c, tensor)
    to_xl_twin = (xl * 4 + yh * 2 + 1 - c, tensor)
    to_yh_twin = (x * 4 + (1 - yh) * 2 + 1 - c, tensor)
    to_core = (q * 2 + (1 - c), tensor)
    to_yl = (dp, (1 - yl) * 4 + z)
    to_zr = (dp, yl * 4 + zr)
    to_zl = (dp, yl * 4 + zl)

    def chip(xx, yy):
        return xx * 2 + yy

    def load(i, src, dst):
        copy = pltpu.make_async_copy(src, dst, load_sem.at[i])
        copy.start()
        return copy

    own_half = pl.ds(pl.multiple_of(c * HALF, 128), HALF)
    sib_half = pl.ds(pl.multiple_of((1 - c) * HALF, 128), HALF)
    load_v = load(0, values, v_in)
    load_s = load(4, scale, scale_in)
    load_g = load(1, gate, gate_in)
    load_u = load(2, up, up_in)

    barrier = pltpu.get_barrier_semaphore()
    for neighbour in (
        to_xr, to_xl, to_yh, to_core, to_yl, to_zr, to_zl, to_xr_twin, to_xl_twin, to_yh_twin
    ):
        pl.semaphore_signal(barrier, inc=1, device_id=neighbour, device_id_type=MESH)
    pl.semaphore_wait(barrier, 10)

    net = Copies(send_sem, recv_sem)
    send, arrived = net.send, net.arrived

    def g_rows(block, first=0, rows=256):
        return g_all.at[c, pl.ds(pl.multiple_of(block * 256 + first, 128), rows)]

    def send_g(block, device, first=0, rows=256):
        ref = g_rows(block, first, rows)
        return send(ref, ref, device)

    load_v.wait()
    load_s.wait()
    own = tensor
    for i in range(2):
        col = jnp.broadcast_to(scale_in[i : i + 1, :], (128, 128)).T
        for k in range(DL // 128):
            part = v_in[i * 128 : (i + 1) * 128, k * 128 : (k + 1) * 128].astype(F32) * col
            g_all[c, pl.ds(pl.multiple_of(own * 256 + i * 128, 128), 128), k * 128 : (k + 1) * 128] = part.astype(BF16)
    a_yl = send_g(own, to_yl)
    a_zr = send_g(own, to_zr)
    a_zl = send_g(own, to_zl)
    s_own = send_g(own, to_core)

    load_g.wait()
    load_u.wait()

    def hidden(half, first, last):
        def tile(k, _):
            cols = pl.ds(pl.multiple_of(half * HALF + k * 128, 128), 128)
            gate_f = gate_in[:, cols].astype(F32)
            h = gate_f * sigmoid(gate_f) * up_in[:, cols].astype(F32)
            h_all[dp, cols, :] = h.T.astype(BF16)
            return 0

        lax.fori_loop(first, last, tile, 0, unroll=True)

    def h_rows(half, first, count):
        return pl.ds(pl.multiple_of(half * HALF + first, 16), count)

    rows1 = h_rows(c, 0, B1)
    rows1a, rows1b = h_rows(c, 0, B1 // 2), h_rows(c, B1 // 2, B1 // 2)
    rows2 = h_rows(c, B1, B2)

    def send_h(first, count, rows, device):
        ref = h_all.at[pl.ds(first, count), rows]
        return send(ref, ref, device)

    twin = 2 * q + 1 - c
    edge = B1 // 128
    hidden(c, edge, HALF // 128)
    b2_xr = [send_h(dp, 1, rows2, to_xr)]
    b2_xl = [send_h(dp, 1, rows2, to_xl)]
    hidden(1 - c, edge, HALF // 128)
    s_h2 = send_h(dp, 1, h_rows(1 - c, B1, B2), to_core)
    hidden(c, 0, edge)
    b1_y = [send_h(dp, 1, rows1, to_yh)]
    b1_xr = [send_h(dp, 1, rows1, to_xr)]
    b1_xl = [send_h(dp, 1, rows1, to_xl)]
    hidden(1 - c, 0, edge)
    s_h1 = send_h(dp, 1, h_rows(1 - c, 0, B1), to_core)
    arrived(s_h2)
    b2_xr.append(send_h(twin, 1, rows2, to_xr))
    b2_xl.append(send_h(twin, 1, rows2, to_xl))
    arrived(s_h1)
    b1_y.append(send_h(twin, 1, rows1, to_yh))
    b1_xr.append(send_h(twin, 1, rows1, to_xr))
    b1_xl.append(send_h(twin, 1, rows1, to_xl))
    b2_y = send_h(2 * q, 2, rows2, to_yh)
    load_w = load(3, weight.at[own_half], w_both.at[c])
    w_sib = send(weight.at[sib_half], w_both.at[c], to_core)

    sib = [send_h(dp, 1, own_half, to_core)]

    def share_h(first, count, rows):
        sib.append(send_h(first, count, rows, to_core))

    def product(block):
        rows = pl.ds(pl.multiple_of(block * 256, 256), 256)

        def cols_of(first, width):
            w_rows = pl.ds(first, width)
            total = lax.dot_general(
                g_all[0, rows, :], w_both[0, w_rows, :], (((1,), (1,)), ((), ())), preferred_element_type=F32
            )
            total += lax.dot_general(
                g_all[1, rows, :], w_both[1, w_rows, :], (((1,), (1,)), ((), ())), preferred_element_type=F32
            )
            return total.astype(BF16)

        for first in range(0, N1, 512):
            p1[block, :, first : first + 512] = cols_of(first, 512)
        p2[block, :, :] = cols_of(N1, N2)

    ql, qr, qf = chip(xl, yh), chip(xr, yh), chip(xf, yh)
    qy, qyl, qyr, qyf = chip(x, 1 - yh), chip(xl, 1 - yh), chip(xr, 1 - yh), chip(xf, 1 - yh)
    other = (1 - yl) * 4 + z
    ol, orr = (1 - yl) * 4 + zl, (1 - yl) * 4 + zr

    for s in b2_xr:
        arrived(s)
    b2_fr = send_h(2 * ql + c, 1, rows2, to_xr)
    b2_yl = send_h(2 * ql, 2, rows2, to_yh)
    for s in b2_xl:
        arrived(s)
    b2_fl = send_h(2 * qr + 1 - c, 1, rows2, to_xl)
    b2_yr = send_h(2 * qr, 2, rows2, to_yh)

    arrived(a_yl)
    a_yzr = send_g(other, to_zr)
    a_yzl = send_g(other, to_zl)
    s_other = send_g(other, to_core)
    arrived(a_zr)
    a_fr = send_g(yl * 4 + zl, to_zr, 0, 128)
    s_zl = send_g(yl * 4 + zl, to_core)
    arrived(a_zl)
    a_fl = send_g(yl * 4 + zr, to_zl, 128, 128)
    s_zr = send_g(yl * 4 + zr, to_core)
    share_h(2 * ql, 2, rows2)
    share_h(2 * qr, 2, rows2)

    load_w.wait()
    arrived(w_sib)
    arrived(s_own)
    arrived(s_other)

    def near(i, _):
        product(i * 4 + z)
        return 0

    lax.fori_loop(0, 2, near, 0)

    for s in b1_xr:
        arrived(s)
    b1_fr = [send_h(2 * ql + c, 1, rows1a, to_xr)]
    for s in b1_xl:
        arrived(s)
    b1_fl = [send_h(2 * qr + 1 - c, 1, rows1a, to_xl)]

    arrived(a_yzr)
    a_yfr = send_g(ol, to_zr, 0, 128)
    s_ol = send_g(ol, to_core)
    arrived(a_yzl)
    a_yfl = send_g(orr, to_zl, 128, 128)
    s_or = send_g(orr, to_core)

    for s in b1_y:
        arrived(s)
    b1_yxr = send_h(2 * qy, 2, rows1, to_xr)
    b1_yxl = send_h(2 * qy, 2, rows1, to_xl)
    b1_fr.append(send_h(2 * ql + c, 1, rows1b, to_xr))
    b1_fl.append(send_h(2 * qr + 1 - c, 1, rows1b, to_xl))
    share_h(2 * ql, 2, rows1)
    share_h(2 * qr, 2, rows1)
    share_h(2 * qy, 2, rows1)

    arrived(b2_fr)
    arrived(b2_fl)
    b2_yf = send_h(2 * qf, 2, rows2, to_yh)
    share_h(2 * qf, 2, rows2)

    for s in (s_zl, s_zr, s_ol, s_or):
        arrived(s)

    def middle(i, _):
        product((i // 2) * 4 + wrap(z - 1 + 2 * lax.rem(i, 2)))
        return 0

    lax.fori_loop(0, 4, middle, 0)

    arrived(a_fr)
    arrived(a_fl)
    s_f = send_g(yl * 4 + zf, to_core)
    arrived(a_yfr)
    arrived(a_yfl)
    s_of = send_g((1 - yl) * 4 + zf, to_core)

    arrived(b1_yxr)
    b1_yfr = send_h(2 * qyl, 1, rows1, to_xr)
    arrived(b1_yxl)
    b1_yfl = send_h(2 * qyr + 1, 1, rows1, to_xl)

    arrived(s_f)
    arrived(s_of)

    def far(i, _):
        product(i * 4 + zf)
        return 0

    lax.fori_loop(0, 2, far, 0)

    own_at = pl.multiple_of(c * 128, 128)
    sib_at = pl.multiple_of((1 - c) * 128, 128)
    own_rows, sib_rows = pl.ds(own_at, 128), pl.ds(sib_at, 128)
    c1 = [[], []]

    def step1(place, yy):
        block = chip(xf, yy)
        return (
            send(p1.at[block, own_rows], r1a.at[0, place], to_xr),
            send(p1.at[block, sib_rows], r1a.at[1, place], to_xl),
        )

    def step2(place, yy, own, right):
        rows = own_rows if own else sib_rows
        block = chip(xr if right else xl, yy)
        if place == 0:
            dst, device = r1b.at[0 if right else 1, rows], to_xr if right else to_xl
        elif own:
            dst, device = s1.at[1 if right else 2, c], to_xr if right else to_xl
        else:
            dst, device = s1.at[1 if right else 2, c], to_xr_twin if right else to_xl_twin
        c1[place].append(send(p1.at[block, rows], dst, device))

    def step2_ready(place, yy):
        step2(place, yy, False, True)
        step2(place, yy, True, False)

    def add(dst, rows, others):
        def strip(i, _):
            at = pl.ds(pl.multiple_of(rows[0] + i * 16, 16), 16)
            total = dst[at, :].astype(F32)
            for other_ref, shift in others:
                total += other_ref[pl.ds(pl.multiple_of(rows[0] - shift + i * 16, 16), 16), :].astype(F32)
            dst[at, :] = total.astype(BF16)
            return 0

        lax.fori_loop(0, rows[1] // 16, strip, 0, unroll=2)

    def step2_rest(place, yy, first):
        arrived(first[0])
        add(p1.at[chip(xr, yy)], (own_at, 128), [(r1a.at[0, place], own_at)])
        step2(place, yy, True, True)
        arrived(first[1])
        add(p1.at[chip(xl, yy)], (sib_at, 128), [(r1a.at[1, place], sib_at)])
        step2(place, yy, False, False)

    first0 = step1(0, 1 - yh)
    c2y_f = send(p2.at[chip(xf, 1 - yh)], r2y.at[xf], to_yh)
    step2_ready(0, 1 - yh)
    c2y_r = send(p2.at[chip(xr, 1 - yh)], r2y.at[xr], to_yh)
    c2y_l = send(p2.at[chip(xl, 1 - yh)], r2y.at[xl], to_yh)
    first1 = step1(1, yh)
    c2y_o = send(p2.at[chip(x, 1 - yh)], r2y.at[x], to_yh)
    keep1 = load(5, p1.at[q, own_rows], s1.at[0, c])
    c1_core = send(p1.at[q, sib_rows], s1.at[0, c], to_core)

    for s in b1_fr + b1_fl:
        arrived(s)
    share_h(2 * qf, 2, rows1)
    arrived(b2_y)
    share_h(2 * qy, 2, rows2)
    arrived(b2_yl)
    share_h(2 * qyl, 2, rows2)
    arrived(b2_yr)
    share_h(2 * qyr, 2, rows2)
    share_h(2 * qyl, 2, rows1)
    share_h(2 * qyr, 2, rows1)
    arrived(b1_yfr)
    arrived(b1_yfl)
    share_h(2 * qyf, 2, rows1)
    arrived(b2_yf)
    share_h(2 * qyf, 2, rows2)

    step2_rest(0, 1 - yh, first0)
    step2_ready(1, yh)

    def dg_tile(m, _):
        rows = pl.ds(pl.multiple_of(m * 256, 256), 256)
        lhs = jnp.concatenate([h_all[s, rows, :] for s in range(16)], axis=1)
        dg[rows, :] = jnp.dot(lhs, g_all[c], preferred_element_type=F32).astype(BF16)
        return 0

    def down(first, last):
        lax.fori_loop(first, last, dg_tile, 0)

    for s in sib:
        arrived(s)
    arrived(c2y_f)
    bf = chip(xf, yh)
    add(p2.at[bf], (0, 256), [(r2y.at[xf], 0)])
    c2a_r = send(p2.at[bf, own_rows], r2a.at[0], to_xr)
    c2a_l = send(p2.at[bf, sib_rows], r2a.at[1], to_xl)
    down(0, 2)
    step2_rest(1, yh, first1)
    down(2, 5)
    for s in c1[0]:
        arrived(s)
    bo = chip(x, 1 - yh)
    add(p1.at[bo], (sib_at, 128), [(r1b.at[0], 0), (r1b.at[1], 0)])
    c1_ys = send(p1.at[bo, sib_rows], s1.at[3, c], to_yh_twin)
    add(p1.at[bo], (own_at, 128), [(r1b.at[0], 0), (r1b.at[1], 0)])
    c1_yo = send(p1.at[bo, own_rows], s1.at[3, c], to_yh)
    br, bl = chip(xr, yh), chip(xl, yh)
    arrived(c2y_r)
    add(p2.at[br], (sib_at, 128), [(r2y.at[xr], 0)])
    c2 = [send(p2.at[br, sib_rows], s2.at[1, c], to_xr_twin)]
    down(5, 8)
    arrived(c2y_l)
    add(p2.at[bl], (own_at, 128), [(r2y.at[xl], 0)])
    c2.append(send(p2.at[bl, own_rows], s2.at[2, c], to_xl))
    down(8, 10)
    arrived(c2a_r)
    add(p2.at[br], (own_at, 128), [(r2y.at[xr], 0), (r2a.at[0], own_at)])
    c2.append(send(p2.at[br, own_rows], s2.at[1, c], to_xr))
    arrived(c2a_l)
    add(p2.at[bl], (sib_at, 128), [(r2y.at[xl], 0), (r2a.at[1], sib_at)])
    c2.append(send(p2.at[bl, sib_rows], s2.at[2, c], to_xl_twin))
    arrived(c2y_o)
    add(p2.at[q], (0, 256), [(r2y.at[x], 0)])
    keep2 = load(6, p2.at[q, own_rows], s2.at[0, c])
    c2_core = send(p2.at[q, sib_rows], s2.at[0, c], to_core)
    down(10, 13)

    keep1.wait()
    keep2.wait()
    for s in [c1_core, c2_core, c1_ys, c1_yo] + c1[1] + c2:
        arrived(s)
    net.finish()


BANDS = 13
SLOTS = 6


def writer(dg, s1, s2, gate, up, dg_out, gg_out, ug_out, buf, gg, ug, buf_sem, out_sem):
    rows = FFL // BANDS

    def band(k):
        slot = k % SLOTS
        return pltpu.make_async_copy(buf.at[slot], dg_out.at[pl.ds(k * rows, rows)], buf_sem.at[slot])

    def finish(half, k):
        cols = slice(half * HALF + k * 128, half * HALF + (k + 1) * 128)
        first, terms = k * 128, s1
        if first >= N1:
            first, terms = first - N1, s2
        grad = terms[0, half, :, first : first + 128].astype(F32)
        for i in range(1, terms.shape[0]):
            grad += terms[i, half, :, first : first + 128].astype(F32)
        gate_f = gate[:, cols].astype(F32)
        s = sigmoid(gate_f)
        gg[:, cols] = (grad * up[:, cols].astype(F32) * s * (1.0 + gate_f * (1.0 - s))).astype(BF16)
        ug[:, cols] = (grad * (gate_f * s)).astype(BF16)

    tiles = [(half, k) for half in range(2) for k in range(HALF // 128)]
    outs = []
    for k in range(BANDS):
        if k >= SLOTS:
            for tile in tiles[:5]:
                finish(*tile)
            del tiles[:5]
            if not tiles and not outs:
                outs = [
                    pltpu.make_async_copy(gg, gg_out, out_sem.at[0]),
                    pltpu.make_async_copy(ug, ug_out, out_sem.at[1]),
                ]
                for out in outs:
                    out.start()
            band(k - SLOTS).wait()
        buf[k % SLOTS] = dg[k * rows : (k + 1) * rows, :].astype(F32)
        band(k).start()
    for k in range(BANDS - SLOTS, BANDS):
        band(k).wait()
    for out in outs:
        out.wait()


def body(grad_values, row_scale, gate_input, up_input, down_weight):
    any_spec = pl.BlockSpec(memory_space=pl.ANY)
    vmem_spec = pl.BlockSpec(memory_space=pltpu.VMEM)
    held = pl.pallas_call(
        kernel,
        out_shape=(
            pltpu.VMEM((FFL, DL), BF16),
            pltpu.VMEM((4, 2, 128, N1), BF16),
            pltpu.VMEM((3, 2, 128, N2), BF16),
            pltpu.VMEM((128, FFL), BF16),
            pltpu.VMEM((128, FFL), BF16),
        ),
        in_specs=[any_spec] * 5,
        out_specs=(vmem_spec,) * 5,
        scratch_shapes=[
            pltpu.VMEM((2, TOK, DL), BF16),
            pltpu.VMEM((2, HALF, DL), BF16),
            pltpu.VMEM((16, FFL, 128), BF16),
            pltpu.VMEM((8, 256, N1), BF16),
            pltpu.VMEM((8, 256, N2), BF16),
            pltpu.VMEM((2, 2, 128, N1), BF16),
            pltpu.VMEM((2, 256, N1), BF16),
            pltpu.VMEM((4, 256, N2), BF16),
            pltpu.VMEM((2, 128, N2), BF16),
            pltpu.VMEM((256, DL), BF16),
            pltpu.VMEM((2, 128), F32),
            pltpu.SemaphoreType.DMA((N_COPIES,)),
            pltpu.SemaphoreType.DMA((N_COPIES,)),
            pltpu.SemaphoreType.DMA((7,)),
        ],
        compiler_params=pltpu.CompilerParams(
            collective_id=0, has_side_effects=True, vmem_limit_bytes=46 * 2**20
        ),
        cost_estimate=pl.CostEstimate(flops=4 * TOK * FFL * DL, bytes_accessed=24 * 2**20, transcendentals=128 * FFL),
    )(grad_values, row_scale.reshape(2, 128), gate_input, up_input, down_weight)
    return pl.pallas_call(
        writer,
        out_shape=(
            jax.ShapeDtypeStruct((FFL, DL), F32),
            jax.ShapeDtypeStruct((128, FFL), BF16),
            jax.ShapeDtypeStruct((128, FFL), BF16),
        ),
        in_specs=[vmem_spec] * 5,
        out_specs=(any_spec,) * 3,
        scratch_shapes=[
            pltpu.VMEM((SLOTS, FFL // BANDS, DL), F32),
            pltpu.VMEM((128, FFL), BF16),
            pltpu.VMEM((128, FFL), BF16),
            pltpu.SemaphoreType.DMA((SLOTS,)),
            pltpu.SemaphoreType.DMA((2,)),
        ],
        compiler_params=pltpu.CompilerParams(vmem_limit_bytes=20 * 2**20),
        cost_estimate=pl.CostEstimate(flops=20 * 128 * FFL, bytes_accessed=24 * 2**20, transcendentals=128 * FFL),
    )(*held)


def solution(mesh):
    return jax.shard_map(
        body,
        mesh=mesh,
        in_specs=(
            P("tensor", "dp"),
            P("tensor"),
            P("dp", "tensor"),
            P("dp", "tensor"),
            P("tensor", "dp"),
        ),
        out_specs=(P("tensor", "dp"), P("dp", "tensor"), P("dp", "tensor")),
        check_vma=False,
    )
```

```python
import functools

import jax
import jax.numpy as jnp
from jax import lax
from jax.experimental import pallas as pl
from jax.experimental.pallas import tpu as pltpu
from jax.sharding import PartitionSpec as P

MESH = pl.DeviceIdType.MESH
BF16 = jnp.bfloat16
F32 = jnp.float32

TOK = 2048
FFL = 3328
HALF = FFL // 2
DL = 1024
N1 = 1024
N2 = HALF - N1
B1 = 1024
B2 = HALF - B1
N_COPIES = 128


def sigmoid(v):
    return 0.5 * jnp.tanh(0.5 * v) + 0.5


class Copies:
    def __init__(self, send_sem, recv_sem):
        self.send_sem, self.recv_sem = send_sem, recv_sem
        self.sent = []

    def send(self, src, dst, device):
        index = len(self.sent)
        copy = pltpu.make_async_remote_copy(
            src_ref=src,
            dst_ref=dst,
            send_sem=self.send_sem.at[index],
            recv_sem=self.recv_sem.at[index],
            device_id=device,
            device_id_type=MESH,
        )
        copy.start()
        self.sent.append(copy)
        return index

    def arrived(self, index):
        self.sent[index].wait_recv()

    def finish(self):
        for copy in self.sent:
            copy.wait_send()


def kernel(
    values, scale, gate, up, weight,
    dg, s1, s2, gate_in, up_in,
    g_all, w_both, h_all, p1, p2, r1a, r1b, r2y, r2a, v_in, scale_in,
    send_sem, recv_sem, load_sem,
):
    dp = lax.axis_index("dp")
    tensor = lax.axis_index("tensor")
    c = lax.rem(dp, 2)
    yh = lax.rem(dp // 2, 2)
    x = dp // 4
    yl = tensor // 4
    z = lax.rem(tensor, 4)
    q = dp // 2

    def wrap(i):
        return lax.rem(i + 4, 4)

    xr, xl, xf = wrap(x + 1), wrap(x - 1), wrap(x + 2)
    zr, zl, zf = wrap(z + 1), wrap(z - 1), wrap(z + 2)
    to_xr = (xr * 4 + yh * 2 + c, tensor)
    to_xl = (xl * 4 + yh * 2 + c, tensor)
    to_yh = (x * 4 + (1 - yh) * 2 + c, tensor)
    to_xr_twin = (xr * 4 + yh * 2 + 1 - c, tensor)
    to_xl_twin = (xl * 4 + yh * 2 + 1 - c, tensor)
    to_yh_twin = (x * 4 + (1 - yh) * 2 + 1 - c, tensor)
    to_core = (q * 2 + (1 - c), tensor)
    to_yl = (dp, (1 - yl) * 4 + z)
    to_zr = (dp, yl * 4 + zr)
    to_zl = (dp, yl * 4 + zl)

    def chip(xx, yy):
        return xx * 2 + yy

    def load(i, src, dst):
        copy = pltpu.make_async_copy(src, dst, load_sem.at[i])
        copy.start()
        return copy

    own_half = pl.ds(pl.multiple_of(c * HALF, 128), HALF)
    sib_half = pl.ds(pl.multiple_of((1 - c) * HALF, 128), HALF)
    load_v = load(0, values, v_in)
    load_s = load(4, scale, scale_in)
    load_g = load(1, gate, gate_in)
    load_u = load(2, up, up_in)

    barrier = pltpu.get_barrier_semaphore()
    for neighbour in (
        to_xr, to_xl, to_yh, to_core, to_yl, to_zr, to_zl, to_xr_twin, to_xl_twin, to_yh_twin
    ):
        pl.semaphore_signal(barrier, inc=1, device_id=neighbour, device_id_type=MESH)
    pl.semaphore_wait(barrier, 10)

    net = Copies(send_sem, recv_sem)
    send, arrived = net.send, net.arrived

    def g_rows(block, first=0, rows=256):
        return g_all.at[c, pl.ds(pl.multiple_of(block * 256 + first, 128), rows)]

    def send_g(block, device, first=0, rows=256):
        ref = g_rows(block, first, rows)
        return send(ref, ref, device)

    load_v.wait()
    load_s.wait()
    own = tensor
    for i in range(2):
        col = jnp.broadcast_to(scale_in[i : i + 1, :], (128, 128)).T
        for k in range(DL // 128):
            part = v_in[i * 128 : (i + 1) * 128, k * 128 : (k + 1) * 128].astype(F32) * col
            g_all[c, pl.ds(pl.multiple_of(own * 256 + i * 128, 128), 128), k * 128 : (k + 1) * 128] = part.astype(BF16)
    a_yl = [send_g(own, to_yl, first, 128) for first in (0, 128)]
    a_zr = send_g(own, to_zr)
    a_zl = send_g(own, to_zl)
    s_own = send_g(own, to_core)

    load_g.wait()
    load_u.wait()

    def hidden(half, first, last):
        def tile(k, _):
            cols = pl.ds(pl.multiple_of(half * HALF + k * 128, 128), 128)
            gate_f = gate_in[:, cols].astype(F32)
            h = gate_f * sigmoid(gate_f) * up_in[:, cols].astype(F32)
            h_all[dp, cols, :] = h.T.astype(BF16)
            return 0

        lax.fori_loop(first, last, tile, 0, unroll=True)

    def h_rows(half, first, count):
        return pl.ds(pl.multiple_of(half * HALF + first, 16), count)

    rows1 = h_rows(c, 0, B1)
    rows1a, rows1b = h_rows(c, 0, B1 // 2), h_rows(c, B1 // 2, B1 // 2)
    rows2 = h_rows(c, B1, B2)

    def send_h(first, count, rows, device):
        ref = h_all.at[pl.ds(first, count), rows]
        return send(ref, ref, device)

    twin = 2 * q + 1 - c
    edge = B1 // 128
    hidden(c, edge, HALF // 128)
    b2_xr = [send_h(dp, 1, rows2, to_xr)]
    b2_xl = [send_h(dp, 1, rows2, to_xl)]
    hidden(1 - c, edge, HALF // 128)
    s_h2 = send_h(dp, 1, h_rows(1 - c, B1, B2), to_core)
    hidden(c, 0, edge)
    b1_y = [send_h(dp, 1, rows1, to_yh)]
    b1_xr = [send_h(dp, 1, rows1, to_xr)]
    b1_xl = [send_h(dp, 1, rows1, to_xl)]
    hidden(1 - c, 0, edge)
    s_h1 = send_h(dp, 1, h_rows(1 - c, 0, B1), to_core)
    arrived(s_h2)
    b2_xr.append(send_h(twin, 1, rows2, to_xr))
    b2_xl.append(send_h(twin, 1, rows2, to_xl))
    arrived(s_h1)
    b1_y.append(send_h(twin, 1, rows1, to_yh))
    b1_xr.append(send_h(twin, 1, rows1, to_xr))
    b1_xl.append(send_h(twin, 1, rows1, to_xl))
    b2_y = send_h(2 * q, 2, rows2, to_yh)
    load_w = load(3, weight.at[own_half], w_both.at[c])
    w_sib = send(weight.at[sib_half], w_both.at[c], to_core)

    sib = [send_h(dp, 1, own_half, to_core)]

    def share_h(first, count, rows):
        sib.append(send_h(first, count, rows, to_core))

    def product(block):
        rows = pl.ds(pl.multiple_of(block * 256, 256), 256)

        def cols_of(first, width):
            w_rows = pl.ds(first, width)
            total = lax.dot_general(
                g_all[0, rows, :], w_both[0, w_rows, :], (((1,), (1,)), ((), ())), preferred_element_type=F32
            )
            total += lax.dot_general(
                g_all[1, rows, :], w_both[1, w_rows, :], (((1,), (1,)), ((), ())), preferred_element_type=F32
            )
            return total.astype(BF16)

        for first in range(0, N1, 512):
            p1[block, :, first : first + 512] = cols_of(first, 512)
        p2[block, :, :] = cols_of(N1, N2)

    ql, qr, qf = chip(xl, yh), chip(xr, yh), chip(xf, yh)
    qy, qyl, qyr, qyf = chip(x, 1 - yh), chip(xl, 1 - yh), chip(xr, 1 - yh), chip(xf, 1 - yh)
    other = (1 - yl) * 4 + z
    ol, orr = (1 - yl) * 4 + zl, (1 - yl) * 4 + zr

    a_yzr, a_yzl = [], []
    for first, s in zip((0, 128), a_yl):
        arrived(s)
        a_yzr.append(send_g(other, to_zr, first, 128))
        a_yzl.append(send_g(other, to_zl, first, 128))
    s_other = send_g(other, to_core)
    arrived(a_zr)
    a_fr = send_g(yl * 4 + zl, to_zr, 0, 128)
    s_zl = send_g(yl * 4 + zl, to_core)
    arrived(a_zl)
    a_fl = send_g(yl * 4 + zr, to_zl, 128, 128)
    s_zr = send_g(yl * 4 + zr, to_core)
    for s in b2_xr:
        arrived(s)
    b2_fr = send_h(2 * ql + c, 1, rows2, to_xr)
    b2_yl = send_h(2 * ql, 2, rows2, to_yh)
    for s in b2_xl:
        arrived(s)
    b2_fl = send_h(2 * qr + 1 - c, 1, rows2, to_xl)
    b2_yr = send_h(2 * qr, 2, rows2, to_yh)

    share_h(2 * ql, 2, rows2)
    share_h(2 * qr, 2, rows2)

    load_w.wait()
    arrived(w_sib)
    arrived(s_own)
    arrived(s_other)

    def near(i, _):
        product(i * 4 + z)
        return 0

    lax.fori_loop(0, 2, near, 0)

    for s in b1_xr:
        arrived(s)
    b1_fr = [send_h(2 * ql + c, 1, rows1a, to_xr)]
    for s in b1_xl:
        arrived(s)
    b1_fl = [send_h(2 * qr + 1 - c, 1, rows1a, to_xl)]

    for s in a_yzr:
        arrived(s)
    a_yfr = send_g(ol, to_zr, 0, 128)
    s_ol = send_g(ol, to_core)
    for s in a_yzl:
        arrived(s)
    a_yfl = send_g(orr, to_zl, 128, 128)
    s_or = send_g(orr, to_core)

    for s in b1_y:
        arrived(s)
    b1_yxr = send_h(2 * qy, 2, rows1, to_xr)
    b1_yxl = send_h(2 * qy, 2, rows1, to_xl)
    b1_fr.append(send_h(2 * ql + c, 1, rows1b, to_xr))
    b1_fl.append(send_h(2 * qr + 1 - c, 1, rows1b, to_xl))
    share_h(2 * ql, 2, rows1)
    share_h(2 * qr, 2, rows1)
    share_h(2 * qy, 2, rows1)

    arrived(b2_fr)
    arrived(b2_fl)
    b2_yf = send_h(2 * qf, 2, rows2, to_yh)
    share_h(2 * qf, 2, rows2)

    for s in (s_zl, s_zr, s_ol, s_or):
        arrived(s)

    def middle(i, _):
        product((i // 2) * 4 + wrap(z - 1 + 2 * lax.rem(i, 2)))
        return 0

    lax.fori_loop(0, 4, middle, 0)

    arrived(a_fr)
    arrived(a_fl)
    s_f = send_g(yl * 4 + zf, to_core)
    arrived(a_yfr)
    arrived(a_yfl)
    s_of = send_g((1 - yl) * 4 + zf, to_core)

    arrived(b1_yxr)
    b1_yfr = send_h(2 * qyl, 1, rows1, to_xr)
    arrived(b1_yxl)
    b1_yfl = send_h(2 * qyr + 1, 1, rows1, to_xl)

    arrived(s_f)
    arrived(s_of)

    def far(i, _):
        product(i * 4 + zf)
        return 0

    lax.fori_loop(0, 2, far, 0)

    own_at = pl.multiple_of(c * 128, 128)
    sib_at = pl.multiple_of((1 - c) * 128, 128)
    own_rows, sib_rows = pl.ds(own_at, 128), pl.ds(sib_at, 128)
    c1 = [[], []]

    def step1(place, yy):
        block = chip(xf, yy)
        return (
            send(p1.at[block, own_rows], r1a.at[0, place], to_xr),
            send(p1.at[block, sib_rows], r1a.at[1, place], to_xl),
        )

    def step2(place, yy, own, right):
        rows = own_rows if own else sib_rows
        block = chip(xr if right else xl, yy)
        if place == 0:
            dst, device = r1b.at[0 if right else 1, rows], to_xr if right else to_xl
        elif own:
            dst, device = s1.at[1 if right else 2, c], to_xr if right else to_xl
        else:
            dst, device = s1.at[1 if right else 2, c], to_xr_twin if right else to_xl_twin
        c1[place].append(send(p1.at[block, rows], dst, device))

    def step2_ready(place, yy):
        step2(place, yy, False, True)
        step2(place, yy, True, False)

    def add(dst, rows, others):
        def strip(i, _):
            at = pl.ds(pl.multiple_of(rows[0] + i * 16, 16), 16)
            total = dst[at, :].astype(F32)
            for other_ref, shift in others:
                total += other_ref[pl.ds(pl.multiple_of(rows[0] - shift + i * 16, 16), 16), :].astype(F32)
            dst[at, :] = total.astype(BF16)
            return 0

        lax.fori_loop(0, rows[1] // 16, strip, 0, unroll=2)

    def step2_rest(place, yy, first):
        arrived(first[0])
        add(p1.at[chip(xr, yy)], (own_at, 128), [(r1a.at[0, place], own_at)])
        step2(place, yy, True, True)
        arrived(first[1])
        add(p1.at[chip(xl, yy)], (sib_at, 128), [(r1a.at[1, place], sib_at)])
        step2(place, yy, False, False)

    first0 = step1(0, 1 - yh)
    c2y_f = send(p2.at[chip(xf, 1 - yh)], r2y.at[xf], to_yh)
    step2_ready(0, 1 - yh)
    c2y_r = send(p2.at[chip(xr, 1 - yh)], r2y.at[xr], to_yh)
    c2y_l = send(p2.at[chip(xl, 1 - yh)], r2y.at[xl], to_yh)
    first1 = step1(1, yh)
    c2y_o = send(p2.at[chip(x, 1 - yh)], r2y.at[x], to_yh)
    keep1 = load(5, p1.at[q, own_rows], s1.at[0, c])
    c1_core = send(p1.at[q, sib_rows], s1.at[0, c], to_core)

    for s in b1_fr + b1_fl:
        arrived(s)
    share_h(2 * qf, 2, rows1)
    arrived(b2_y)
    share_h(2 * qy, 2, rows2)
    arrived(b2_yl)
    share_h(2 * qyl, 2, rows2)
    arrived(b2_yr)
    share_h(2 * qyr, 2, rows2)
    share_h(2 * qyl, 2, rows1)
    share_h(2 * qyr, 2, rows1)
    arrived(b1_yfr)
    arrived(b1_yfl)
    share_h(2 * qyf, 2, rows1)
    arrived(b2_yf)
    share_h(2 * qyf, 2, rows2)

    step2_rest(0, 1 - yh, first0)
    step2_ready(1, yh)

    def dg_tile(m, _):
        rows = pl.ds(pl.multiple_of(m * 256, 256), 256)
        lhs = jnp.concatenate([h_all[s, rows, :] for s in range(16)], axis=1)
        dg[rows, :] = jnp.dot(lhs, g_all[c], preferred_element_type=F32).astype(BF16)
        return 0

    def down(first, last):
        lax.fori_loop(first, last, dg_tile, 0)

    for s in sib:
        arrived(s)
    arrived(c2y_f)
    bf = chip(xf, yh)
    add(p2.at[bf], (0, 256), [(r2y.at[xf], 0)])
    c2a_r = send(p2.at[bf, own_rows], r2a.at[0], to_xr)
    c2a_l = send(p2.at[bf, sib_rows], r2a.at[1], to_xl)
    down(0, 2)
    step2_rest(1, yh, first1)
    down(2, 5)
    for s in c1[0]:
        arrived(s)
    bo = chip(x, 1 - yh)
    add(p1.at[bo], (sib_at, 128), [(r1b.at[0], 0), (r1b.at[1], 0)])
    c1_ys = send(p1.at[bo, sib_rows], s1.at[3, c], to_yh_twin)
    add(p1.at[bo], (own_at, 128), [(r1b.at[0], 0), (r1b.at[1], 0)])
    c1_yo = send(p1.at[bo, own_rows], s1.at[3, c], to_yh)
    br, bl = chip(xr, yh), chip(xl, yh)
    arrived(c2y_r)
    add(p2.at[br], (sib_at, 128), [(r2y.at[xr], 0)])
    c2 = [send(p2.at[br, sib_rows], s2.at[1, c], to_xr_twin)]
    down(5, 8)
    arrived(c2y_l)
    add(p2.at[bl], (own_at, 128), [(r2y.at[xl], 0)])
    c2.append(send(p2.at[bl, own_rows], s2.at[2, c], to_xl))
    down(8, 10)
    arrived(c2a_r)
    add(p2.at[br], (own_at, 128), [(r2y.at[xr], 0), (r2a.at[0], own_at)])
    c2.append(send(p2.at[br, own_rows], s2.at[1, c], to_xr))
    arrived(c2a_l)
    add(p2.at[bl], (sib_at, 128), [(r2y.at[xl], 0), (r2a.at[1], sib_at)])
    c2.append(send(p2.at[bl, sib_rows], s2.at[2, c], to_xl_twin))
    arrived(c2y_o)
    add(p2.at[q], (0, 256), [(r2y.at[x], 0)])
    keep2 = load(6, p2.at[q, own_rows], s2.at[0, c])
    c2_core = send(p2.at[q, sib_rows], s2.at[0, c], to_core)
    down(10, 13)

    keep1.wait()
    keep2.wait()
    for s in [c1_core, c2_core, c1_ys, c1_yo] + c1[1] + c2:
        arrived(s)
    net.finish()


BANDS = 13
SLOTS = 6


def writer(dg, s1, s2, gate, up, dg_out, gg_out, ug_out, buf, gg, ug, buf_sem, out_sem):
    rows = FFL // BANDS

    def band(k):
        slot = k % SLOTS
        return pltpu.make_async_copy(buf.at[slot], dg_out.at[pl.ds(k * rows, rows)], buf_sem.at[slot])

    def finish(half, k):
        cols = slice(half * HALF + k * 128, half * HALF + (k + 1) * 128)
        first, terms = k * 128, s1
        if first >= N1:
            first, terms = first - N1, s2
        grad = terms[0, half, :, first : first + 128].astype(F32)
        for i in range(1, terms.shape[0]):
            grad += terms[i, half, :, first : first + 128].astype(F32)
        gate_f = gate[:, cols].astype(F32)
        s = sigmoid(gate_f)
        gg[:, cols] = (grad * up[:, cols].astype(F32) * s * (1.0 + gate_f * (1.0 - s))).astype(BF16)
        ug[:, cols] = (grad * (gate_f * s)).astype(BF16)

    tiles = [(half, k) for half in range(2) for k in range(HALF // 128)]
    outs = []
    for k in range(BANDS):
        if k >= SLOTS:
            for tile in tiles[:5]:
                finish(*tile)
            del tiles[:5]
            if not tiles and not outs:
                outs = [
                    pltpu.make_async_copy(gg, gg_out, out_sem.at[0]),
                    pltpu.make_async_copy(ug, ug_out, out_sem.at[1]),
                ]
                for out in outs:
                    out.start()
            band(k - SLOTS).wait()
        buf[k % SLOTS] = dg[k * rows : (k + 1) * rows, :].astype(F32)
        band(k).start()
    for k in range(BANDS - SLOTS, BANDS):
        band(k).wait()
    for out in outs:
        out.wait()


def body(grad_values, row_scale, gate_input, up_input, down_weight):
    any_spec = pl.BlockSpec(memory_space=pl.ANY)
    vmem_spec = pl.BlockSpec(memory_space=pltpu.VMEM)
    held = pl.pallas_call(
        kernel,
        out_shape=(
            pltpu.VMEM((FFL, DL), BF16),
            pltpu.VMEM((4, 2, 128, N1), BF16),
            pltpu.VMEM((3, 2, 128, N2), BF16),
            pltpu.VMEM((128, FFL), BF16),
            pltpu.VMEM((128, FFL), BF16),
        ),
        in_specs=[any_spec] * 5,
        out_specs=(vmem_spec,) * 5,
        scratch_shapes=[
            pltpu.VMEM((2, TOK, DL), BF16),
            pltpu.VMEM((2, HALF, DL), BF16),
            pltpu.VMEM((16, FFL, 128), BF16),
            pltpu.VMEM((8, 256, N1), BF16),
            pltpu.VMEM((8, 256, N2), BF16),
            pltpu.VMEM((2, 2, 128, N1), BF16),
            pltpu.VMEM((2, 256, N1), BF16),
            pltpu.VMEM((4, 256, N2), BF16),
            pltpu.VMEM((2, 128, N2), BF16),
            pltpu.VMEM((256, DL), BF16),
            pltpu.VMEM((2, 128), F32),
            pltpu.SemaphoreType.DMA((N_COPIES,)),
            pltpu.SemaphoreType.DMA((N_COPIES,)),
            pltpu.SemaphoreType.DMA((7,)),
        ],
        compiler_params=pltpu.CompilerParams(
            collective_id=0, has_side_effects=True, vmem_limit_bytes=46 * 2**20
        ),
        cost_estimate=pl.CostEstimate(flops=4 * TOK * FFL * DL, bytes_accessed=24 * 2**20, transcendentals=128 * FFL),
    )(grad_values, row_scale.reshape(2, 128), gate_input, up_input, down_weight)
    return pl.pallas_call(
        writer,
        out_shape=(
            jax.ShapeDtypeStruct((FFL, DL), F32),
            jax.ShapeDtypeStruct((128, FFL), BF16),
            jax.ShapeDtypeStruct((128, FFL), BF16),
        ),
        in_specs=[vmem_spec] * 5,
        out_specs=(any_spec,) * 3,
        scratch_shapes=[
            pltpu.VMEM((SLOTS, FFL // BANDS, DL), F32),
            pltpu.VMEM((128, FFL), BF16),
            pltpu.VMEM((128, FFL), BF16),
            pltpu.SemaphoreType.DMA((SLOTS,)),
            pltpu.SemaphoreType.DMA((2,)),
        ],
        compiler_params=pltpu.CompilerParams(vmem_limit_bytes=20 * 2**20),
        cost_estimate=pl.CostEstimate(flops=20 * 128 * FFL, bytes_accessed=24 * 2**20, transcendentals=128 * FFL),
    )(*held)


def solution(mesh):
    return jax.shard_map(
        body,
        mesh=mesh,
        in_specs=(
            P("tensor", "dp"),
            P("tensor"),
            P("dp", "tensor"),
            P("dp", "tensor"),
            P("tensor", "dp"),
        ),
        out_specs=(P("tensor", "dp"), P("dp", "tensor"), P("dp", "tensor")),
        check_vma=False,
    )
```

```python
import functools

import jax
import jax.numpy as jnp
from jax import lax
from jax.experimental import pallas as pl
from jax.experimental.pallas import tpu as pltpu
from jax.sharding import PartitionSpec as P

MESH = pl.DeviceIdType.MESH
BF16 = jnp.bfloat16
F32 = jnp.float32

TOK = 2048
FFL = 3328
HALF = FFL // 2
DL = 1024
N1 = 1024
N2 = HALF - N1
B1 = 1024
B2 = HALF - B1
N_COPIES = 128


def sigmoid(v):
    return 0.5 * jnp.tanh(0.5 * v) + 0.5


class Copies:
    def __init__(self, send_sem, recv_sem):
        self.send_sem, self.recv_sem = send_sem, recv_sem
        self.sent = []

    def send(self, src, dst, device):
        index = len(self.sent)
        copy = pltpu.make_async_remote_copy(
            src_ref=src,
            dst_ref=dst,
            send_sem=self.send_sem.at[index],
            recv_sem=self.recv_sem.at[index],
            device_id=device,
            device_id_type=MESH,
        )
        copy.start()
        self.sent.append(copy)
        return index

    def arrived(self, index):
        self.sent[index].wait_recv()

    def finish(self):
        for copy in self.sent:
            copy.wait_send()


def kernel(
    values, scale, gate, up, weight,
    dg, s1, s2, gate_in, up_in,
    g_all, w_both, h_all, p1, p2, r1a, r1b, r2y, r2a, v_in, scale_in,
    send_sem, recv_sem, load_sem,
):
    dp = lax.axis_index("dp")
    tensor = lax.axis_index("tensor")
    c = lax.rem(dp, 2)
    yh = lax.rem(dp // 2, 2)
    x = dp // 4
    yl = tensor // 4
    z = lax.rem(tensor, 4)
    q = dp // 2

    def wrap(i):
        return lax.rem(i + 4, 4)

    xr, xl, xf = wrap(x + 1), wrap(x - 1), wrap(x + 2)
    zr, zl, zf = wrap(z + 1), wrap(z - 1), wrap(z + 2)
    to_xr = (xr * 4 + yh * 2 + c, tensor)
    to_xl = (xl * 4 + yh * 2 + c, tensor)
    to_yh = (x * 4 + (1 - yh) * 2 + c, tensor)
    to_xr_twin = (xr * 4 + yh * 2 + 1 - c, tensor)
    to_xl_twin = (xl * 4 + yh * 2 + 1 - c, tensor)
    to_yh_twin = (x * 4 + (1 - yh) * 2 + 1 - c, tensor)
    to_core = (q * 2 + (1 - c), tensor)
    to_yl = (dp, (1 - yl) * 4 + z)
    to_zr = (dp, yl * 4 + zr)
    to_zl = (dp, yl * 4 + zl)

    def chip(xx, yy):
        return xx * 2 + yy

    def load(i, src, dst):
        copy = pltpu.make_async_copy(src, dst, load_sem.at[i])
        copy.start()
        return copy

    own_half = pl.ds(pl.multiple_of(c * HALF, 128), HALF)
    sib_half = pl.ds(pl.multiple_of((1 - c) * HALF, 128), HALF)
    load_v = load(0, values, v_in)
    load_s = load(4, scale, scale_in)
    load_g = load(1, gate, gate_in)
    load_u = load(2, up, up_in)

    barrier = pltpu.get_barrier_semaphore()
    for neighbour in (
        to_xr, to_xl, to_yh, to_core, to_yl, to_zr, to_zl, to_xr_twin, to_xl_twin, to_yh_twin
    ):
        pl.semaphore_signal(barrier, inc=1, device_id=neighbour, device_id_type=MESH)

    net = Copies(send_sem, recv_sem)
    send, arrived = net.send, net.arrived

    def g_rows(block, first=0, rows=256):
        return g_all.at[c, pl.ds(pl.multiple_of(block * 256 + first, 128), rows)]

    def send_g(block, device, first=0, rows=256):
        ref = g_rows(block, first, rows)
        return send(ref, ref, device)

    load_v.wait()
    load_s.wait()
    own = tensor
    for i in range(2):
        col = jnp.broadcast_to(scale_in[i : i + 1, :], (128, 128)).T
        for k in range(DL // 128):
            part = v_in[i * 128 : (i + 1) * 128, k * 128 : (k + 1) * 128].astype(F32) * col
            g_all[c, pl.ds(pl.multiple_of(own * 256 + i * 128, 128), 128), k * 128 : (k + 1) * 128] = part.astype(BF16)
    pl.semaphore_wait(barrier, 10)
    a_yl = [send_g(own, to_yl, first, 128) for first in (0, 128)]
    a_zr = send_g(own, to_zr)
    a_zl = send_g(own, to_zl)
    s_own = send_g(own, to_core)

    load_g.wait()
    load_u.wait()

    def hidden(half, first, last):
        def tile(k, _):
            cols = pl.ds(pl.multiple_of(half * HALF + k * 128, 128), 128)
            gate_f = gate_in[:, cols].astype(F32)
            h = gate_f * sigmoid(gate_f) * up_in[:, cols].astype(F32)
            h_all[dp, cols, :] = h.T.astype(BF16)
            return 0

        lax.fori_loop(first, last, tile, 0, unroll=True)

    def h_rows(half, first, count):
        return pl.ds(pl.multiple_of(half * HALF + first, 16), count)

    rows1 = h_rows(c, 0, B1)
    rows1a, rows1b = h_rows(c, 0, B1 // 2), h_rows(c, B1 // 2, B1 // 2)
    rows2 = h_rows(c, B1, B2)

    def send_h(first, count, rows, device):
        ref = h_all.at[pl.ds(first, count), rows]
        return send(ref, ref, device)

    twin = 2 * q + 1 - c
    edge = B1 // 128
    hidden(c, edge, HALF // 128)
    b2_xr = [send_h(dp, 1, rows2, to_xr)]
    b2_xl = [send_h(dp, 1, rows2, to_xl)]
    hidden(1 - c, edge, HALF // 128)
    s_h2 = send_h(dp, 1, h_rows(1 - c, B1, B2), to_core)
    hidden(c, 0, edge)
    b1_y = [send_h(dp, 1, rows1, to_yh)]
    b1_xr = [send_h(dp, 1, rows1, to_xr)]
    b1_xl = [send_h(dp, 1, rows1, to_xl)]
    hidden(1 - c, 0, edge)
    s_h1 = send_h(dp, 1, h_rows(1 - c, 0, B1), to_core)
    arrived(s_h2)
    b2_xr.append(send_h(twin, 1, rows2, to_xr))
    b2_xl.append(send_h(twin, 1, rows2, to_xl))
    arrived(s_h1)
    b1_y.append(send_h(twin, 1, rows1, to_yh))
    b1_xr.append(send_h(twin, 1, rows1, to_xr))
    b1_xl.append(send_h(twin, 1, rows1, to_xl))
    b2_y = send_h(2 * q, 2, rows2, to_yh)
    load_w = load(3, weight.at[own_half], w_both.at[c])
    w_sib = send(weight.at[sib_half], w_both.at[c], to_core)

    sib = [send_h(dp, 1, own_half, to_core)]

    def share_h(first, count, rows):
        sib.append(send_h(first, count, rows, to_core))

    def product(block):
        rows = pl.ds(pl.multiple_of(block * 256, 256), 256)

        def cols_of(first, width):
            w_rows = pl.ds(first, width)
            total = lax.dot_general(
                g_all[0, rows, :], w_both[0, w_rows, :], (((1,), (1,)), ((), ())), preferred_element_type=F32
            )
            total += lax.dot_general(
                g_all[1, rows, :], w_both[1, w_rows, :], (((1,), (1,)), ((), ())), preferred_element_type=F32
            )
            return total.astype(BF16)

        for first in range(0, N1, 512):
            p1[block, :, first : first + 512] = cols_of(first, 512)
        p2[block, :, :] = cols_of(N1, N2)

    ql, qr, qf = chip(xl, yh), chip(xr, yh), chip(xf, yh)
    qy, qyl, qyr, qyf = chip(x, 1 - yh), chip(xl, 1 - yh), chip(xr, 1 - yh), chip(xf, 1 - yh)
    other = (1 - yl) * 4 + z
    ol, orr = (1 - yl) * 4 + zl, (1 - yl) * 4 + zr

    a_yzr, a_yzl = [], []
    for first, s in zip((0, 128), a_yl):
        arrived(s)
        a_yzr.append(send_g(other, to_zr, first, 128))
        a_yzl.append(send_g(other, to_zl, first, 128))
    s_other = send_g(other, to_core)
    arrived(a_zr)
    a_fr = send_g(yl * 4 + zl, to_zr, 0, 128)
    s_zl = send_g(yl * 4 + zl, to_core)
    arrived(a_zl)
    a_fl = send_g(yl * 4 + zr, to_zl, 128, 128)
    s_zr = send_g(yl * 4 + zr, to_core)
    for s in b2_xr:
        arrived(s)
    b2_fr = send_h(2 * ql + c, 1, rows2, to_xr)
    b2_yl = send_h(2 * ql, 2, rows2, to_yh)
    for s in b2_xl:
        arrived(s)
    b2_fl = send_h(2 * qr + 1 - c, 1, rows2, to_xl)
    b2_yr = send_h(2 * qr, 2, rows2, to_yh)

    share_h(2 * ql, 2, rows2)
    share_h(2 * qr, 2, rows2)

    load_w.wait()
    arrived(w_sib)
    arrived(s_own)
    arrived(s_other)

    def near(i, _):
        product(i * 4 + z)
        return 0

    lax.fori_loop(0, 2, near, 0)

    for s in b1_xr:
        arrived(s)
    b1_fr = [send_h(2 * ql + c, 1, rows1a, to_xr)]
    for s in b1_xl:
        arrived(s)
    b1_fl = [send_h(2 * qr + 1 - c, 1, rows1a, to_xl)]

    def products(y_lo):
        def middle(i, _):
            product(y_lo * 4 + wrap(z - 1 + 2 * i))
            return 0

        lax.fori_loop(0, 2, middle, 0)

    arrived(s_zl)
    arrived(s_zr)
    products(yl)

    for s in a_yzr:
        arrived(s)
    a_yfr = send_g(ol, to_zr, 0, 128)
    s_ol = send_g(ol, to_core)
    for s in a_yzl:
        arrived(s)
    a_yfl = send_g(orr, to_zl, 128, 128)
    s_or = send_g(orr, to_core)

    for s in b1_y:
        arrived(s)
    b1_yxr = send_h(2 * qy, 2, rows1, to_xr)
    b1_yxl = send_h(2 * qy, 2, rows1, to_xl)
    b1_fr.append(send_h(2 * ql + c, 1, rows1b, to_xr))
    b1_fl.append(send_h(2 * qr + 1 - c, 1, rows1b, to_xl))
    share_h(2 * ql, 2, rows1)
    share_h(2 * qr, 2, rows1)
    share_h(2 * qy, 2, rows1)

    arrived(b2_fr)
    arrived(b2_fl)
    b2_yf = send_h(2 * qf, 2, rows2, to_yh)
    share_h(2 * qf, 2, rows2)

    arrived(s_ol)
    arrived(s_or)
    products(1 - yl)

    arrived(a_fr)
    arrived(a_fl)
    s_f = send_g(yl * 4 + zf, to_core)
    arrived(a_yfr)
    arrived(a_yfl)
    s_of = send_g((1 - yl) * 4 + zf, to_core)

    arrived(b1_yxr)
    b1_yfr = send_h(2 * qyl, 1, rows1, to_xr)
    arrived(b1_yxl)
    b1_yfl = send_h(2 * qyr + 1, 1, rows1, to_xl)

    arrived(s_f)
    arrived(s_of)

    def far(i, _):
        product(i * 4 + zf)
        return 0

    lax.fori_loop(0, 2, far, 0)

    own_at = pl.multiple_of(c * 128, 128)
    sib_at = pl.multiple_of((1 - c) * 128, 128)
    own_rows, sib_rows = pl.ds(own_at, 128), pl.ds(sib_at, 128)
    c1 = [[], []]

    def step1(place, yy):
        block = chip(xf, yy)
        return (
            send(p1.at[block, own_rows], r1a.at[0, place], to_xr),
            send(p1.at[block, sib_rows], r1a.at[1, place], to_xl),
        )

    def step2(place, yy, own, right):
        rows = own_rows if own else sib_rows
        block = chip(xr if right else xl, yy)
        if place == 0:
            dst, device = r1b.at[0 if right else 1, rows], to_xr if right else to_xl
        elif own:
            dst, device = s1.at[1 if right else 2, c], to_xr if right else to_xl
        else:
            dst, device = s1.at[1 if right else 2, c], to_xr_twin if right else to_xl_twin
        c1[place].append(send(p1.at[block, rows], dst, device))

    def step2_ready(place, yy):
        step2(place, yy, False, True)
        step2(place, yy, True, False)

    def add(dst, rows, others):
        def strip(i, _):
            at = pl.ds(pl.multiple_of(rows[0] + i * 16, 16), 16)
            total = dst[at, :].astype(F32)
            for other_ref, shift in others:
                total += other_ref[pl.ds(pl.multiple_of(rows[0] - shift + i * 16, 16), 16), :].astype(F32)
            dst[at, :] = total.astype(BF16)
            return 0

        lax.fori_loop(0, rows[1] // 16, strip, 0, unroll=2)

    def step2_rest(place, yy, first):
        arrived(first[0])
        add(p1.at[chip(xr, yy)], (own_at, 128), [(r1a.at[0, place], own_at)])
        step2(place, yy, True, True)
        arrived(first[1])
        add(p1.at[chip(xl, yy)], (sib_at, 128), [(r1a.at[1, place], sib_at)])
        step2(place, yy, False, False)

    first0 = step1(0, 1 - yh)
    c2y_f = send(p2.at[chip(xf, 1 - yh)], r2y.at[xf], to_yh)
    step2_ready(0, 1 - yh)
    c2y_r = send(p2.at[chip(xr, 1 - yh)], r2y.at[xr], to_yh)
    c2y_l = send(p2.at[chip(xl, 1 - yh)], r2y.at[xl], to_yh)
    first1 = step1(1, yh)
    c2y_o = send(p2.at[chip(x, 1 - yh)], r2y.at[x], to_yh)
    keep1 = load(5, p1.at[q, own_rows], s1.at[0, c])
    c1_core = send(p1.at[q, sib_rows], s1.at[0, c], to_core)

    for s in b1_fr + b1_fl:
        arrived(s)
    share_h(2 * qf, 2, rows1)
    arrived(b2_y)
    share_h(2 * qy, 2, rows2)
    arrived(b2_yl)
    share_h(2 * qyl, 2, rows2)
    arrived(b2_yr)
    share_h(2 * qyr, 2, rows2)
    share_h(2 * qyl, 2, rows1)
    share_h(2 * qyr, 2, rows1)
    arrived(b1_yfr)
    arrived(b1_yfl)
    share_h(2 * qyf, 2, rows1)
    arrived(b2_yf)
    share_h(2 * qyf, 2, rows2)

    step2_rest(0, 1 - yh, first0)
    step2_ready(1, yh)

    def dg_tile(m, _):
        rows = pl.ds(pl.multiple_of(m * 256, 256), 256)
        lhs = jnp.concatenate([h_all[s, rows, :] for s in range(16)], axis=1)
        dg[rows, :] = jnp.dot(lhs, g_all[c], preferred_element_type=F32).astype(BF16)
        return 0

    def down(first, last):
        lax.fori_loop(first, last, dg_tile, 0)

    for s in sib:
        arrived(s)
    arrived(c2y_f)
    bf = chip(xf, yh)
    add(p2.at[bf], (0, 256), [(r2y.at[xf], 0)])
    c2a_r = send(p2.at[bf, own_rows], r2a.at[0], to_xr)
    c2a_l = send(p2.at[bf, sib_rows], r2a.at[1], to_xl)
    down(0, 2)
    step2_rest(1, yh, first1)
    down(2, 5)
    for s in c1[0]:
        arrived(s)
    bo = chip(x, 1 - yh)
    add(p1.at[bo], (sib_at, 128), [(r1b.at[0], 0), (r1b.at[1], 0)])
    c1_ys = send(p1.at[bo, sib_rows], s1.at[3, c], to_yh_twin)
    add(p1.at[bo], (own_at, 128), [(r1b.at[0], 0), (r1b.at[1], 0)])
    c1_yo = send(p1.at[bo, own_rows], s1.at[3, c], to_yh)
    br, bl = chip(xr, yh), chip(xl, yh)
    arrived(c2y_r)
    add(p2.at[br], (sib_at, 128), [(r2y.at[xr], 0)])
    c2 = [send(p2.at[br, sib_rows], s2.at[1, c], to_xr_twin)]
    down(5, 8)
    arrived(c2y_l)
    add(p2.at[bl], (own_at, 128), [(r2y.at[xl], 0)])
    c2.append(send(p2.at[bl, own_rows], s2.at[2, c], to_xl))
    down(8, 10)
    arrived(c2a_r)
    add(p2.at[br], (own_at, 128), [(r2y.at[xr], 0), (r2a.at[0], own_at)])
    c2.append(send(p2.at[br, own_rows], s2.at[1, c], to_xr))
    arrived(c2a_l)
    add(p2.at[bl], (sib_at, 128), [(r2y.at[xl], 0), (r2a.at[1], sib_at)])
    c2.append(send(p2.at[bl, sib_rows], s2.at[2, c], to_xl_twin))
    arrived(c2y_o)
    add(p2.at[q], (0, 256), [(r2y.at[x], 0)])
    keep2 = load(6, p2.at[q, own_rows], s2.at[0, c])
    c2_core = send(p2.at[q, sib_rows], s2.at[0, c], to_core)
    down(10, 13)

    keep1.wait()
    keep2.wait()
    for s in [c1_core, c2_core, c1_ys, c1_yo] + c1[1] + c2:
        arrived(s)
    net.finish()


BANDS = 13
SLOTS = 6


def writer(dg, s1, s2, gate, up, dg_out, gg_out, ug_out, buf, gg, ug, buf_sem, out_sem):
    rows = FFL // BANDS

    def band(k):
        slot = k % SLOTS
        return pltpu.make_async_copy(buf.at[slot], dg_out.at[pl.ds(k * rows, rows)], buf_sem.at[slot])

    def finish(half, k):
        cols = slice(half * HALF + k * 128, half * HALF + (k + 1) * 128)
        first, terms = k * 128, s1
        if first >= N1:
            first, terms = first - N1, s2
        grad = terms[0, half, :, first : first + 128].astype(F32)
        for i in range(1, terms.shape[0]):
            grad += terms[i, half, :, first : first + 128].astype(F32)
        gate_f = gate[:, cols].astype(F32)
        s = sigmoid(gate_f)
        gg[:, cols] = (grad * up[:, cols].astype(F32) * s * (1.0 + gate_f * (1.0 - s))).astype(BF16)
        ug[:, cols] = (grad * (gate_f * s)).astype(BF16)

    tiles = [(half, k) for half in range(2) for k in range(HALF // 128)]
    outs = []
    for k in range(BANDS):
        if k >= SLOTS:
            for tile in tiles[:5]:
                finish(*tile)
            del tiles[:5]
            if not tiles and not outs:
                outs = [
                    pltpu.make_async_copy(gg, gg_out, out_sem.at[0]),
                    pltpu.make_async_copy(ug, ug_out, out_sem.at[1]),
                ]
                for out in outs:
                    out.start()
            band(k - SLOTS).wait()
        buf[k % SLOTS] = dg[k * rows : (k + 1) * rows, :].astype(F32)
        band(k).start()
    for k in range(BANDS - SLOTS, BANDS):
        band(k).wait()
    for out in outs:
        out.wait()


def body(grad_values, row_scale, gate_input, up_input, down_weight):
    any_spec = pl.BlockSpec(memory_space=pl.ANY)
    vmem_spec = pl.BlockSpec(memory_space=pltpu.VMEM)
    held = pl.pallas_call(
        kernel,
        out_shape=(
            pltpu.VMEM((FFL, DL), BF16),
            pltpu.VMEM((4, 2, 128, N1), BF16),
            pltpu.VMEM((3, 2, 128, N2), BF16),
            pltpu.VMEM((128, FFL), BF16),
            pltpu.VMEM((128, FFL), BF16),
        ),
        in_specs=[any_spec] * 5,
        out_specs=(vmem_spec,) * 5,
        scratch_shapes=[
            pltpu.VMEM((2, TOK, DL), BF16),
            pltpu.VMEM((2, HALF, DL), BF16),
            pltpu.VMEM((16, FFL, 128), BF16),
            pltpu.VMEM((8, 256, N1), BF16),
            pltpu.VMEM((8, 256, N2), BF16),
            pltpu.VMEM((2, 2, 128, N1), BF16),
            pltpu.VMEM((2, 256, N1), BF16),
            pltpu.VMEM((4, 256, N2), BF16),
            pltpu.VMEM((2, 128, N2), BF16),
            pltpu.VMEM((256, DL), BF16),
            pltpu.VMEM((2, 128), F32),
            pltpu.SemaphoreType.DMA((N_COPIES,)),
            pltpu.SemaphoreType.DMA((N_COPIES,)),
            pltpu.SemaphoreType.DMA((7,)),
        ],
        compiler_params=pltpu.CompilerParams(
            collective_id=0, has_side_effects=True, vmem_limit_bytes=46 * 2**20
        ),
        cost_estimate=pl.CostEstimate(flops=4 * TOK * FFL * DL, bytes_accessed=24 * 2**20, transcendentals=128 * FFL),
    )(grad_values, row_scale.reshape(2, 128), gate_input, up_input, down_weight)
    return pl.pallas_call(
        writer,
        out_shape=(
            jax.ShapeDtypeStruct((FFL, DL), F32),
            jax.ShapeDtypeStruct((128, FFL), BF16),
            jax.ShapeDtypeStruct((128, FFL), BF16),
        ),
        in_specs=[vmem_spec] * 5,
        out_specs=(any_spec,) * 3,
        scratch_shapes=[
            pltpu.VMEM((SLOTS, FFL // BANDS, DL), F32),
            pltpu.VMEM((128, FFL), BF16),
            pltpu.VMEM((128, FFL), BF16),
            pltpu.SemaphoreType.DMA((SLOTS,)),
            pltpu.SemaphoreType.DMA((2,)),
        ],
        compiler_params=pltpu.CompilerParams(vmem_limit_bytes=20 * 2**20),
        cost_estimate=pl.CostEstimate(flops=20 * 128 * FFL, bytes_accessed=24 * 2**20, transcendentals=128 * FFL),
    )(*held)


def solution(mesh):
    return jax.shard_map(
        body,
        mesh=mesh,
        in_specs=(
            P("tensor", "dp"),
            P("tensor"),
            P("dp", "tensor"),
            P("dp", "tensor"),
            P("tensor", "dp"),
        ),
        out_specs=(P("tensor", "dp"), P("dp", "tensor"), P("dp", "tensor")),
        check_vma=False,
    )
```
